32 devices in a mesh: section: 4 (over y, x), row: 2 (over core), col: 4 (over z).
Axes of the slice: x: 2, y: 2, z: 4, core: 2. Of those that a mesh axis runs over, the one named last changes fastest.
Arguments:
- latent: bfloat16 [2, 32, 64, 128], P(None, 'row', 'col'), may hold values from -6 to 6
- hidden_old: bfloat16 [4, 2, 32, 64, 128], P('section', None, 'row', 'col'), may hold values from -1 to 1
- cell_old: float32 [4, 2, 32, 64, 128], P('section', None, 'row', 'col'), may hold values from -6 to 6
- weights: bfloat16 [4, 9, 256, 512], P('section'), may hold values from -0.125 to 0.125
- bias: float32 [4, 512], P('section'), may hold values from -3 to 3
Outputs:
- hidden_new: bfloat16 [4, 2, 32, 64, 128], P('section', None, 'row', 'col')
- cell_new: float32 [4, 2, 32, 64, 128], P('section', None, 'row', 'col')
The draws below stay inside these ranges and needn't reach their ends.
All inputs are finite; a program needn't handle non-finite values.
Results may differ from the reference program's by a relative error of at most 0.0016.
Values may be sent and summed in bfloat16 or wider, within the bound.
A program may use at most 64 MiB of HBM per device.

```python
import jax
import jax.numpy as jnp

HIDDEN_SIZE = 128
GATES = 512
LAYERS = 4
BATCH = 2
GRID_H = 32
GRID_W = 64


def block_scale(own_key, dims, pieces, least, high):
    def one(position, blocks):
        heights = jax.random.uniform(jax.random.fold_in(jax.random.fold_in(own_key, 6), position), (blocks,), jnp.float32, least / len(pieces), high / len(pieces))
        return jnp.repeat(jnp.exp(heights), dims[position] // blocks).reshape((-1,) + (1,) * (len(dims) - position - 1))

    gain = one(*pieces[0])
    for cut in pieces[1:]:
        gain = gain * one(*cut)
    return gain


def bell_draw(rng, extent, scale, most, cuts=(), kind=jnp.bfloat16):
    entries = jax.random.normal(rng, extent, jnp.float32) * scale
    if len(cuts) > 0:
        entries = block_scale(rng, extent, cuts, -0.22, 0.18) * entries
    return jnp.clip(entries, min=-most, max=most).astype(kind)


def setup_inputs(seed: int = 0) -> dict:
    arg_keys = jax.random.split(jax.random.key(seed), 6)
    latent = bell_draw(arg_keys[0], (BATCH, GRID_H, GRID_W, HIDDEN_SIZE), 1.0, 6.0, ((1, 2), (2, 4)))
    hidden_old = jnp.clip(jax.random.uniform(arg_keys[1], (LAYERS, BATCH, GRID_H, GRID_W, HIDDEN_SIZE), jnp.float32, -1.0, 1.0) * block_scale(arg_keys[1], (LAYERS, BATCH, GRID_H, GRID_W, HIDDEN_SIZE), ((0, 4), (2, 2), (3, 4)), -0.4, 0.0), -1.0, 1.0).astype(jnp.bfloat16)
    cell_old = bell_draw(arg_keys[2], (LAYERS, BATCH, GRID_H, GRID_W, HIDDEN_SIZE), 1.0, 6.0, ((0, 4), (2, 2), (3, 4)), jnp.float32)
    weights = bell_draw(arg_keys[3], (LAYERS, 9, 2 * HIDDEN_SIZE, GATES), (18 * HIDDEN_SIZE) ** -0.5, 0.125, ((0, 4),))
    bias = bell_draw(arg_keys[4], (LAYERS, GATES), 0.5, 3.0, ((0, 4),), jnp.float32)
    return {"latent": latent, "hidden_old": hidden_old, "cell_old": cell_old, "weights": weights, "bias": bias}


def conv_layer(layer_in, hidden_prev, cell_prev, kernel, offset):
    stacked = jnp.concatenate([layer_in, hidden_prev], axis=-1)
    padded = jnp.pad(stacked, ((0, 0), (1, 1), (1, 1), (0, 0)))
    batch, height, width, chans = stacked.shape
    gates = jnp.zeros((batch * height * width, kernel.shape[-1]), jnp.float32)
    for tap in range(9):
        dy = tap // 3
        dx = tap % 3
        window = padded[:, dy:dy + height, dx:dx + width, :].reshape(-1, chans)
        gates = gates + jnp.dot(window, kernel[tap], preferred_element_type=jnp.float32)
    gates = (gates + offset[None, :]).reshape(batch, height, width, -1)
    quarter = gates.shape[-1] // 4
    gate_i = jax.nn.sigmoid(gates[..., :quarter])
    gate_f = jax.nn.sigmoid(gates[..., quarter:2 * quarter])
    gate_g = jnp.tanh(gates[..., 2 * quarter:3 * quarter])
    gate_o = jax.nn.sigmoid(gates[..., 3 * quarter:])
    cell = gate_f * cell_prev + gate_i * gate_g
    hidden = (gate_o * jnp.tanh(cell)).astype(jnp.bfloat16)
    return hidden, cell


def reference(latent, hidden_old, cell_old, weights, bias):
    layer_in = latent
    hiddens = []
    cells = []
    for layer in range(LAYERS):
        hidden, cell = conv_layer(layer_in, hidden_old[layer], cell_old[layer], weights[layer], bias[layer])
        hiddens.append(hidden)
        cells.append(cell)
        layer_in = hidden
    return jnp.stack(hiddens), jnp.stack(cells)
```

```python
import functools

import jax
import jax.numpy as jnp
from jax import lax
from jax.experimental import pallas as pl
from jax.experimental.pallas import tpu as pltpu
from jax.sharding import PartitionSpec as P

MESH = pl.DeviceIdType.MESH
F32 = jnp.float32
BF16 = jnp.bfloat16
AROUND = tuple((dr, dc) for dr in (-1, 0, 1) for dc in (-1, 0, 1) if (dr, dc) != (0, 0))
PAD = 8


def opposite(d):
    return len(AROUND) - 1 - d


def sigmoid(x):
    return 0.5 * jnp.tanh(0.5 * x) + 0.5


def kernel(
    sizes,
    latent_hbm,
    hidden_hbm,
    cell_hbm,
    weights_hbm,
    bias_ref,
    hidden_out,
    cell_out,
    latent,
    hidden,
    cell,
    w_in,
    w_own,
    main_in,
    halo_in,
    halo_own,
    own_edges,
    lat_edges,
    new_edges,
    new_hidden,
    new_cell,
    wide,
    taps,
    gates,
    load_sem,
    store_sem,
    own_send,
    own_recv,
    lat_send,
    in_recv,
    edge_send,
    main_send,
    main_recv,
):
    sections, rows, cols = sizes
    batch, height, width, chans = latent.shape
    half = height // 2
    s = lax.axis_index("section")
    r = lax.axis_index("row")
    c = lax.axis_index("col")
    first = s == 0
    feeds = s + 1 < sections

    def inside(dr, dc):
        return (r + dr >= 0) & (r + dr < rows) & (c + dc >= 0) & (c + dc < cols)

    def at(ds, dr, dc):
        return (s + ds, r + dr, c + dc)

    loads = [
        pltpu.make_async_copy(src, dst, load_sem.at[k])
        for k, (src, dst) in enumerate(
            (
                (hidden_hbm.at[0], hidden),
                (latent_hbm, latent),
                (weights_hbm.at[0, :, pl.ds(chans, chans)], w_own),
                (weights_hbm.at[0, :, pl.ds(0, chans)], w_in),
                (cell_hbm.at[0], cell),
            )
        )
    ]
    for load in loads:
        load.start()

    halo_in[...] = jnp.zeros_like(halo_in)
    halo_own[...] = jnp.zeros_like(halo_own)

    barrier = pltpu.get_barrier_semaphore()
    expected = jnp.int32(0)
    for dr, dc in AROUND + ((0, 0),):
        there = inside(dr, dc)
        if (dr, dc) != (0, 0):

            @pl.when(there)
            def _():
                pl.semaphore_signal(barrier, inc=1, device_id=at(0, dr, dc), device_id_type=MESH)

            expected = expected + there.astype(jnp.int32)

        @pl.when(there & (s > 0))
        def _():
            pl.semaphore_signal(barrier, inc=1, device_id=at(-1, dr, dc), device_id_type=MESH)

        expected = expected + (there & feeds).astype(jnp.int32)

    def pack(source, edges, b):
        tile = source[b].astype(F32)
        edges[0, b] = tile[:, 0, :].astype(BF16)
        edges[1, b] = tile[:, width - 1, :].astype(BF16)

    loads[0].wait()
    for b in range(batch):
        pack(hidden, own_edges, b)
    loads[1].wait()

    @pl.when(first)
    def _():
        for b in range(batch):
            pack(latent, lat_edges, b)

    pl.semaphore_wait(barrier, expected)

    def edge(tile, edges, b, dr, dc):
        if dr == 0:
            return edges.at[0 if dc < 0 else 1, b]
        return tile.at[b, 0 if dr < 0 else height - 1]

    def own_copy(d, b):
        dr, dc = AROUND[d]
        back = opposite(d)
        return pltpu.make_async_remote_copy(
            src_ref=edge(hidden, own_edges, b, dr, dc),
            dst_ref=halo_own.at[back, b],
            send_sem=own_send.at[d, b],
            recv_sem=own_recv.at[back, b],
            device_id=at(0, dr, dc),
            device_id_type=MESH,
        )

    def lat_copy(d, b):
        dr, dc = AROUND[d]
        back = opposite(d)
        return pltpu.make_async_remote_copy(
            src_ref=edge(latent, lat_edges, b, dr, dc),
            dst_ref=halo_in.at[back, b],
            send_sem=lat_send.at[d, b],
            recv_sem=in_recv.at[back, b],
            device_id=at(0, dr, dc),
            device_id_type=MESH,
        )

    def edge_copy(d, b):
        dr, dc = AROUND[d]
        back = opposite(d)
        return pltpu.make_async_remote_copy(
            src_ref=edge(new_hidden, new_edges, b, dr, dc),
            dst_ref=halo_in.at[back, b],
            send_sem=edge_send.at[d, b],
            recv_sem=in_recv.at[back, b],
            device_id=at(1, dr, dc),
            device_id_type=MESH,
        )

    def main_copy(b, part):
        span = pl.ds(part * half, half)
        return pltpu.make_async_remote_copy(
            src_ref=new_hidden.at[b, span],
            dst_ref=main_in.at[b, span],
            send_sem=main_send.at[b, part],
            recv_sem=main_recv.at[b, part],
            device_id=at(1, 0, 0),
            device_id_type=MESH,
        )

    for b in range(batch):
        for d, (dr, dc) in enumerate(AROUND):

            @pl.when(inside(dr, dc))
            def _():
                own_copy(d, b).start()

            @pl.when(inside(dr, dc) & first)
            def _():
                lat_copy(d, b).start()

    def convolved(main, halo, w):
        left, right = PAD - 1, PAD + width
        wide[1 : height + 1, PAD : PAD + width, :] = main.astype(F32)
        for d, (dr, dc) in enumerate(AROUND):
            strip = halo(d).astype(F32)
            line = 0 if dr < 0 else height + 1
            if dr == 0:
                side = left if dc < 0 else right
                wide[1 : height + 1, side : side + 1, :] = strip.reshape(height, 1, chans)
            elif dc == 0:
                wide[line, PAD : PAD + width, :] = strip
            elif dc < 0:
                wide[line, left : left + 1, :] = strip[width - 1 : width]
            else:
                wide[line, right : right + 1, :] = strip[0:1]
        for dx in range(3):
            taps[:, :, dx * chans : (dx + 1) * chans] = wide[
                :, left + dx : left + dx + width, :
            ].astype(BF16)
        patch = jnp.concatenate(
            [
                taps[dy : dy + height].reshape(height * width, 3 * chans)
                for dy in range(3)
            ],
            axis=-1,
        )
        return jnp.dot(patch, w[...].reshape(9 * chans, -1), preferred_element_type=F32)

    stores = []
    for b in range(batch):
        for d, (dr, dc) in enumerate(AROUND):

            @pl.when(inside(dr, dc))
            def _():
                own_copy(opposite(d), b).wait_recv()

        if b == 0:
            loads[2].wait()
        gates[...] = convolved(hidden[b], lambda d: halo_own[d, b], w_own) + bias_ref[...]

        @pl.when(first)
        def _():
            main_in[b] = latent[b]

        for d, (dr, dc) in enumerate(AROUND):

            @pl.when(inside(dr, dc))
            def _():
                edge_copy(opposite(d), b).wait_recv()

        for part in range(2):

            @pl.when(s > 0)
            def _():
                main_copy(b, part).wait_recv()

        if b == 0:
            loads[3].wait()
        gates[...] += convolved(main_in[b], lambda d: halo_in[d, b], w_in)
        if b == 0:
            loads[4].wait()
        for part in range(2):
            span = pl.ds(part * half, half)
            z = gates[part * half * width : (part + 1) * half * width]
            old = cell[b, span].reshape(half * width, chans)
            gate_i = sigmoid(z[:, :chans])
            gate_f = sigmoid(z[:, chans : 2 * chans])
            gate_g = jnp.tanh(z[:, 2 * chans : 3 * chans])
            gate_o = sigmoid(z[:, 3 * chans :])
            now = gate_f * old + gate_i * gate_g
            new_cell[b, span] = now.reshape(half, width, chans)
            out = (gate_o * jnp.tanh(now)).astype(BF16).reshape(half, width, chans)
            new_hidden[b, span] = out
            tile = out.astype(F32)
            new_edges[0, b, span] = tile[:, 0, :].astype(BF16)
            new_edges[1, b, span] = tile[:, width - 1, :].astype(BF16)
            for d, (dr, dc) in enumerate(AROUND):
                if (part == 0) == (dr < 0):

                    @pl.when(inside(dr, dc) & feeds)
                    def _():
                        edge_copy(d, b).start()

            @pl.when(feeds)
            def _():
                main_copy(b, part).start()

        for k, (src, dst) in enumerate(((new_cell, cell_out), (new_hidden, hidden_out))):
            store = pltpu.make_async_copy(src.at[b], dst.at[0, b], store_sem.at[k, b])
            store.start()
            stores.append(store)

    for b in range(batch):
        for d, (dr, dc) in enumerate(AROUND):

            @pl.when(inside(dr, dc))
            def _():
                own_copy(d, b).wait_send()

            @pl.when(inside(dr, dc) & first)
            def _():
                lat_copy(d, b).wait_send()

            @pl.when(inside(dr, dc) & feeds)
            def _():
                edge_copy(d, b).wait_send()

        for part in range(2):

            @pl.when(feeds)
            def _():
                main_copy(b, part).wait_send()

    for store in stores:
        store.wait()


def on_device(latent, hidden_old, cell_old, weights, bias):
    sizes = tuple(lax.axis_size(axis) for axis in ("section", "row", "col"))
    batch, height, width, chans = latent.shape
    gate_chans = weights.shape[-1]
    around = len(AROUND)
    edge = max(height, width)
    assert height == width and height % 16 == 0
    tile = (batch, height, width, chans)
    dma = pltpu.SemaphoreType.DMA
    anywhere = pl.BlockSpec(memory_space=pl.ANY)
    flops = 2 * batch * height * width * 9 * 2 * chans * gate_chans
    return pl.pallas_call(
        functools.partial(kernel, sizes),
        out_shape=(
            jax.ShapeDtypeStruct(hidden_old.shape, BF16),
            jax.ShapeDtypeStruct(cell_old.shape, F32),
        ),
        in_specs=[anywhere] * 4 + [pl.BlockSpec(memory_space=pltpu.VMEM)],
        out_specs=(anywhere, anywhere),
        scratch_shapes=[
            pltpu.VMEM(tile, BF16),
            pltpu.VMEM(tile, BF16),
            pltpu.VMEM(tile, F32),
            pltpu.VMEM((9, chans, gate_chans), BF16),
            pltpu.VMEM((9, chans, gate_chans), BF16),
            pltpu.VMEM(tile, BF16),
            pltpu.VMEM((around, batch, edge, chans), BF16),
            pltpu.VMEM((around, batch, edge, chans), BF16),
            pltpu.VMEM((2, batch, edge, chans), BF16),
            pltpu.VMEM((2, batch, edge, chans), BF16),
            pltpu.VMEM((2, batch, edge, chans), BF16),
            pltpu.VMEM(tile, BF16),
            pltpu.VMEM(tile, F32),
            pltpu.VMEM((height + 2, width + 2 * PAD, chans), F32),
            pltpu.VMEM((height + 2, width, 3 * chans), BF16),
            pltpu.VMEM((height * width, gate_chans), F32),
            dma((5,)),
            dma((2, batch)),
            dma((around, batch)),
            dma((around, batch)),
            dma((around, batch)),
            dma((around, batch)),
            dma((around, batch)),
            dma((batch, 2)),
            dma((batch, 2)),
        ],
        compiler_params=pltpu.CompilerParams(
            collective_id=0, has_side_effects=True, vmem_limit_bytes=32 * 1024 * 1024
        ),
        cost_estimate=pl.CostEstimate(
            flops=flops, bytes_accessed=weights.size * 2, transcendentals=0
        ),
    )(latent, hidden_old, cell_old, weights, bias)


def solution(mesh):
    in_specs = (
        P(None, "row", "col", None),
        P("section", None, "row", "col", None),
        P("section", None, "row", "col", None),
        P("section", None, None, None),
        P("section", None),
    )
    out_specs = (P("section", None, "row", "col", None), P("section", None, "row", "col", None))
    return jax.shard_map(
        on_device, mesh=mesh, in_specs=in_specs, out_specs=out_specs, check_vma=False
    )
```

```python
import functools

import jax
import jax.numpy as jnp
from jax import lax
from jax.experimental import pallas as pl
from jax.experimental.pallas import tpu as pltpu
from jax.sharding import PartitionSpec as P

MESH = pl.DeviceIdType.MESH
F32 = jnp.float32
BF16 = jnp.bfloat16
AROUND = tuple((dr, dc) for dr in (-1, 0, 1) for dc in (-1, 0, 1) if (dr, dc) != (0, 0))
PAD = 8


def opposite(d):
    return len(AROUND) - 1 - d


def sigmoid(x):
    return 0.5 * jnp.tanh(0.5 * x) + 0.5


def kernel(
    sizes,
    latent_hbm,
    hidden_hbm,
    cell_hbm,
    weights_hbm,
    bias_ref,
    hidden_out,
    cell_out,
    latent,
    hidden,
    cell,
    w_in,
    w_own,
    main_in,
    halo_in,
    halo_own,
    own_edges,
    lat_edges,
    new_edges,
    new_hidden,
    new_cell,
    wide,
    taps,
    gates,
    load_sem,
    store_sem,
    own_send,
    own_recv,
    lat_send,
    in_recv,
    edge_send,
    main_send,
    main_recv,
    ready,
):
    sections, rows, cols = sizes
    batch, height, width, chans = latent.shape
    half = height // 2
    s = lax.axis_index("section")
    r = lax.axis_index("row")
    c = lax.axis_index("col")
    first = s == 0
    feeds = s + 1 < sections

    def inside(dr, dc):
        return (r + dr >= 0) & (r + dr < rows) & (c + dc >= 0) & (c + dc < cols)

    def at(ds, dr, dc):
        return (s + ds, r + dr, c + dc)

    loads = [
        pltpu.make_async_copy(src, dst, load_sem.at[k])
        for k, (src, dst) in enumerate(
            (
                (hidden_hbm.at[0], hidden),
                (latent_hbm, latent),
                (weights_hbm.at[0, :, pl.ds(chans, chans)], w_own),
                (weights_hbm.at[0, :, pl.ds(0, chans)], w_in),
                (cell_hbm.at[0], cell),
            )
        )
    ]
    for load in loads:
        load.start()

    halo_in[...] = jnp.zeros_like(halo_in)
    halo_own[...] = jnp.zeros_like(halo_own)

    barrier = pltpu.get_barrier_semaphore()
    expected = jnp.int32(0)
    listeners = jnp.int32(0)
    for dr, dc in AROUND + ((0, 0),):
        there = inside(dr, dc)
        if (dr, dc) != (0, 0):

            @pl.when(there)
            def _():
                pl.semaphore_signal(barrier, inc=1, device_id=at(0, dr, dc), device_id_type=MESH)

            expected = expected + there.astype(jnp.int32)

    for dr, dc in AROUND + ((0, 0),):
        there = inside(dr, dc)

        @pl.when(there & feeds)
        def _():
            pl.semaphore_signal(barrier, inc=1, device_id=at(1, dr, dc), device_id_type=MESH)

        expected = expected + (there & (s > 0)).astype(jnp.int32)
        listeners = listeners + (there & feeds).astype(jnp.int32)

    def pack(source, edges, b):
        tile = source[b].astype(F32)
        edges[0, b] = tile[:, 0, :].astype(BF16)
        edges[1, b] = tile[:, width - 1, :].astype(BF16)

    loads[0].wait()
    for b in range(batch):
        pack(hidden, own_edges, b)
    loads[1].wait()

    @pl.when(first)
    def _():
        for b in range(batch):
            pack(latent, lat_edges, b)

    pl.semaphore_wait(barrier, expected)

    for dr, dc in AROUND + ((0, 0),):

        @pl.when(inside(dr, dc) & (s > 0))
        def _():
            pl.semaphore_signal(ready, inc=1, device_id=at(-1, dr, dc), device_id_type=MESH)

    def edge(tile, edges, b, dr, dc):
        if dr == 0:
            return edges.at[0 if dc < 0 else 1, b]
        return tile.at[b, 0 if dr < 0 else height - 1]

    def own_copy(d, b):
        dr, dc = AROUND[d]
        back = opposite(d)
        return pltpu.make_async_remote_copy(
            src_ref=edge(hidden, own_edges, b, dr, dc),
            dst_ref=halo_own.at[back, b],
            send_sem=own_send.at[d, b],
            recv_sem=own_recv.at[back, b],
            device_id=at(0, dr, dc),
            device_id_type=MESH,
        )

    def lat_copy(d, b):
        dr, dc = AROUND[d]
        back = opposite(d)
        return pltpu.make_async_remote_copy(
            src_ref=edge(latent, lat_edges, b, dr, dc),
            dst_ref=halo_in.at[back, b],
            send_sem=lat_send.at[d, b],
            recv_sem=in_recv.at[back, b],
            device_id=at(0, dr, dc),
            device_id_type=MESH,
        )

    def edge_copy(d, b):
        dr, dc = AROUND[d]
        back = opposite(d)
        return pltpu.make_async_remote_copy(
            src_ref=edge(new_hidden, new_edges, b, dr, dc),
            dst_ref=halo_in.at[back, b],
            send_sem=edge_send.at[d, b],
            recv_sem=in_recv.at[back, b],
            device_id=at(1, dr, dc),
            device_id_type=MESH,
        )

    def main_copy(b, part):
        span = pl.ds(part * half, half)
        return pltpu.make_async_remote_copy(
            src_ref=new_hidden.at[b, span],
            dst_ref=main_in.at[b, span],
            send_sem=main_send.at[b, part],
            recv_sem=main_recv.at[b, part],
            device_id=at(1, 0, 0),
            device_id_type=MESH,
        )

    for b in range(batch):
        for d, (dr, dc) in enumerate(AROUND):

            @pl.when(inside(dr, dc))
            def _():
                own_copy(d, b).start()

            @pl.when(inside(dr, dc) & first)
            def _():
                lat_copy(d, b).start()

    def convolved(main, halo, w):
        left, right = PAD - 1, PAD + width
        wide[1 : height + 1, PAD : PAD + width, :] = main.astype(F32)
        for d, (dr, dc) in enumerate(AROUND):
            strip = halo(d).astype(F32)
            line = 0 if dr < 0 else height + 1
            if dr == 0:
                side = left if dc < 0 else right
                wide[1 : height + 1, side : side + 1, :] = strip.reshape(height, 1, chans)
            elif dc == 0:
                wide[line, PAD : PAD + width, :] = strip
            elif dc < 0:
                wide[line, left : left + 1, :] = strip[width - 1 : width]
            else:
                wide[line, right : right + 1, :] = strip[0:1]
        for dx in range(3):
            taps[:, :, dx * chans : (dx + 1) * chans] = wide[
                :, left + dx : left + dx + width, :
            ].astype(BF16)
        patch = jnp.concatenate(
            [
                taps[dy : dy + height].reshape(height * width, 3 * chans)
                for dy in range(3)
            ],
            axis=-1,
        )
        return jnp.dot(patch, w[...].reshape(9 * chans, -1), preferred_element_type=F32)

    stores = []
    for b in range(batch):
        for d, (dr, dc) in enumerate(AROUND):

            @pl.when(inside(dr, dc))
            def _():
                own_copy(opposite(d), b).wait_recv()

        if b == 0:
            loads[2].wait()
        gates[...] = convolved(hidden[b], lambda d: halo_own[d, b], w_own) + bias_ref[...]

        @pl.when(first)
        def _():
            main_in[b] = latent[b]

        for d, (dr, dc) in enumerate(AROUND):

            @pl.when(inside(dr, dc))
            def _():
                edge_copy(opposite(d), b).wait_recv()

        for part in range(2):

            @pl.when(s > 0)
            def _():
                main_copy(b, part).wait_recv()

        if b == 0:
            loads[3].wait()
        gates[...] += convolved(main_in[b], lambda d: halo_in[d, b], w_in)
        if b == 0:
            loads[4].wait()

            @pl.when(feeds)
            def _():
                pl.semaphore_wait(ready, listeners)

        for part in range(2):
            span = pl.ds(part * half, half)
            z = gates[part * half * width : (part + 1) * half * width]
            old = cell[b, span].reshape(half * width, chans)
            gate_i = sigmoid(z[:, :chans])
            gate_f = sigmoid(z[:, chans : 2 * chans])
            gate_g = jnp.tanh(z[:, 2 * chans : 3 * chans])
            gate_o = sigmoid(z[:, 3 * chans :])
            now = gate_f * old + gate_i * gate_g
            new_cell[b, span] = now.reshape(half, width, chans)
            out = (gate_o * jnp.tanh(now)).astype(BF16).reshape(half, width, chans)
            new_hidden[b, span] = out
            tile = out.astype(F32)
            new_edges[0, b, span] = tile[:, 0, :].astype(BF16)
            new_edges[1, b, span] = tile[:, width - 1, :].astype(BF16)
            for d, (dr, dc) in enumerate(AROUND):
                if (part == 0) == (dr < 0):

                    @pl.when(inside(dr, dc) & feeds)
                    def _():
                        edge_copy(d, b).start()

            @pl.when(feeds)
            def _():
                main_copy(b, part).start()

        for k, (src, dst) in enumerate(((new_cell, cell_out), (new_hidden, hidden_out))):
            store = pltpu.make_async_copy(src.at[b], dst.at[0, b], store_sem.at[k, b])
            store.start()
            stores.append(store)

    for b in range(batch):
        for d, (dr, dc) in enumerate(AROUND):

            @pl.when(inside(dr, dc))
            def _():
                own_copy(d, b).wait_send()

            @pl.when(inside(dr, dc) & first)
            def _():
                lat_copy(d, b).wait_send()

            @pl.when(inside(dr, dc) & feeds)
            def _():
                edge_copy(d, b).wait_send()

        for part in range(2):

            @pl.when(feeds)
            def _():
                main_copy(b, part).wait_send()

    for store in stores:
        store.wait()


def on_device(latent, hidden_old, cell_old, weights, bias):
    sizes = tuple(lax.axis_size(axis) for axis in ("section", "row", "col"))
    batch, height, width, chans = latent.shape
    gate_chans = weights.shape[-1]
    around = len(AROUND)
    edge = max(height, width)
    assert height == width and height % 16 == 0
    tile = (batch, height, width, chans)
    dma = pltpu.SemaphoreType.DMA
    anywhere = pl.BlockSpec(memory_space=pltpu.HBM)
    flops = 2 * batch * height * width * 9 * 2 * chans * gate_chans
    return pl.pallas_call(
        functools.partial(kernel, sizes),
        out_shape=(
            jax.ShapeDtypeStruct(hidden_old.shape, BF16),
            jax.ShapeDtypeStruct(cell_old.shape, F32),
        ),
        in_specs=[anywhere] * 4 + [pl.BlockSpec(memory_space=pltpu.VMEM)],
        out_specs=(anywhere, anywhere),
        scratch_shapes=[
            pltpu.VMEM(tile, BF16),
            pltpu.VMEM(tile, BF16),
            pltpu.VMEM(tile, F32),
            pltpu.VMEM((9, chans, gate_chans), BF16),
            pltpu.VMEM((9, chans, gate_chans), BF16),
            pltpu.VMEM(tile, BF16),
            pltpu.VMEM((around, batch, edge, chans), BF16),
            pltpu.VMEM((around, batch, edge, chans), BF16),
            pltpu.VMEM((2, batch, edge, chans), BF16),
            pltpu.VMEM((2, batch, edge, chans), BF16),
            pltpu.VMEM((2, batch, edge, chans), BF16),
            pltpu.VMEM(tile, BF16),
            pltpu.VMEM(tile, F32),
            pltpu.VMEM((height + 2, width + 2 * PAD, chans), F32),
            pltpu.VMEM((height + 2, width, 3 * chans), BF16),
            pltpu.VMEM((height * width, gate_chans), F32),
            dma((5,)),
            dma((2, batch)),
            dma((around, batch)),
            dma((around, batch)),
            dma((around, batch)),
            dma((around, batch)),
            dma((around, batch)),
            dma((batch, 2)),
            dma((batch, 2)),
            pltpu.SemaphoreType.REGULAR,
        ],
        compiler_params=pltpu.CompilerParams(
            collective_id=0, has_side_effects=True, vmem_limit_bytes=64 * 1024 * 1024 - 4096
        ),
        cost_estimate=pl.CostEstimate(
            flops=flops, bytes_accessed=weights.size * 2, transcendentals=0
        ),
    )(latent, hidden_old, cell_old, weights, bias)


def solution(mesh):
    in_specs = (
        P(None, "row", "col", None),
        P("section", None, "row", "col", None),
        P("section", None, "row", "col", None),
        P("section", None, None, None),
        P("section", None),
    )
    out_specs = (P("section", None, "row", "col", None), P("section", None, "row", "col", None))
    return jax.shard_map(
        on_device, mesh=mesh, in_specs=in_specs, out_specs=out_specs, check_vma=False
    )
```

```python
import functools

import jax
import jax.numpy as jnp
from jax import lax
from jax.experimental import pallas as pl
from jax.experimental.pallas import tpu as pltpu
from jax.sharding import PartitionSpec as P

MESH = pl.DeviceIdType.MESH
F32 = jnp.float32
BF16 = jnp.bfloat16
AROUND = tuple((dr, dc) for dr in (-1, 0, 1) for dc in (-1, 0, 1) if (dr, dc) != (0, 0))
PAD = 8


def opposite(d):
    dr, dc = AROUND[d]
    return AROUND.index((dr, -dc))


def sigmoid(x):
    return 0.5 * jnp.tanh(0.5 * x) + 0.5


def kernel(
    sizes,
    latent_hbm,
    hidden_hbm,
    cell_hbm,
    weights_hbm,
    bias_ref,
    hidden_out,
    cell_out,
    latent,
    hidden,
    cell,
    w_in,
    w_own,
    main_in,
    halo_in,
    halo_own,
    halo_lat,
    own_edges,
    lat_edges,
    new_edges,
    new_hidden,
    out_hidden,
    new_cell,
    wide,
    taps,
    gates,
    load_sem,
    store_sem,
    own_send,
    own_recv,
    lat_send,
    lat_recv,
    in_recv,
    edge_send,
    main_send,
    main_recv,
    ready,
):
    sections, rows, cols = sizes
    batch, height, width, chans = latent.shape
    half = height // 2
    least = half - (sections - 1)
    s = lax.axis_index("section")
    r = lax.axis_index("row")
    c = lax.axis_index("col")
    first = s == 0
    feeds = s + 1 < sections
    odd = lax.rem(r, 2)
    step = 1 - 2 * odd

    def line(y):
        return y + odd * (height - 1 - 2 * y)

    def ordered(source, b, y0, y1):
        return jnp.stack([source[b, line(y)] for y in range(y0, y1)])

    def inside(dr, dc):
        return (r + dr * step >= 0) & (r + dr * step < rows) & (c + dc >= 0) & (c + dc < cols)

    def at(ds, dr, dc):
        return (s + ds, r + dr * step, c + dc)

    def taps_of(dy, start):
        return weights_hbm.at[0, pl.ds(3 * (dy + odd * (2 - 2 * dy)), 3), pl.ds(start, chans)]

    loads = [
        pltpu.make_async_copy(src, dst, load_sem.at[k])
        for k, (src, dst) in enumerate(
            [(hidden_hbm.at[0], hidden), (latent_hbm, latent)]
            + [(taps_of(dy, chans), w_own.at[pl.ds(3 * dy, 3)]) for dy in range(3)]
            + [(taps_of(dy, 0), w_in.at[pl.ds(3 * dy, 3)]) for dy in range(3)]
            + [(cell_hbm.at[0], cell)]
        )
    ]
    for load in loads:
        load.start()

    halo_in[...] = jnp.zeros_like(halo_in)
    halo_own[...] = jnp.zeros_like(halo_own)
    halo_lat[...] = jnp.zeros_like(halo_lat)

    barrier = pltpu.get_barrier_semaphore()
    expected = jnp.int32(0)
    listeners = jnp.int32(0)
    for dr, dc in AROUND + ((0, 0),):
        there = inside(dr, dc)
        if (dr, dc) != (0, 0):

            @pl.when(there)
            def _():
                pl.semaphore_signal(barrier, inc=1, device_id=at(0, dr, dc), device_id_type=MESH)

            expected = expected + there.astype(jnp.int32)

    for dr, dc in AROUND + ((0, 0),):
        there = inside(dr, dc)

        @pl.when(there & feeds)
        def _():
            pl.semaphore_signal(barrier, inc=1, device_id=at(1, dr, dc), device_id_type=MESH)

        expected = expected + (there & (s > 0)).astype(jnp.int32)
        listeners = listeners + (there & feeds).astype(jnp.int32)

    def pack(source, edges, b):
        tile = ordered(source, b, 0, height).astype(F32)
        edges[0, b] = tile[:, 0, :].astype(BF16)
        edges[1, b] = tile[:, width - 1, :].astype(BF16)

    loads[0].wait()
    for b in range(batch):
        pack(hidden, own_edges, b)
    loads[1].wait()

    @pl.when(first)
    def _():
        for b in range(batch):
            pack(latent, lat_edges, b)

    pl.semaphore_wait(barrier, expected)

    for dr, dc in AROUND + ((0, 0),):

        @pl.when(inside(dr, dc) & (s > 0))
        def _():
            pl.semaphore_signal(ready, inc=1, device_id=at(-1, dr, dc), device_id_type=MESH)

    def edge(tile, edges, b, dr, dc):
        if dr == 0:
            return edges.at[0 if dc < 0 else 1, b]
        return tile.at[b, line(0 if dr < 0 else height - 1)]

    def own_copy(d, b):
        dr, dc = AROUND[d]
        back = opposite(d)
        return pltpu.make_async_remote_copy(
            src_ref=edge(hidden, own_edges, b, dr, dc),
            dst_ref=halo_own.at[back, b],
            send_sem=own_send.at[d, b],
            recv_sem=own_recv.at[back, b],
            device_id=at(0, dr, dc),
            device_id_type=MESH,
        )

    def lat_copy(d, b):
        dr, dc = AROUND[d]
        back = opposite(d)
        return pltpu.make_async_remote_copy(
            src_ref=edge(latent, lat_edges, b, dr, dc),
            dst_ref=halo_lat.at[back, b],
            send_sem=lat_send.at[d, b],
            recv_sem=lat_recv.at[back, b],
            device_id=at(0, dr, dc),
            device_id_type=MESH,
        )

    def edge_copy(d, b, part):
        dr, dc = AROUND[d]
        back = opposite(d)
        if dr == 0:
            src = new_edges.at[0 if dc < 0 else 1, b, part]
        else:
            src = new_hidden.at[b, 0 if dr < 0 else height - 1]
        return pltpu.make_async_remote_copy(
            src_ref=src,
            dst_ref=halo_in.at[back, b, part],
            send_sem=edge_send.at[d, b, part],
            recv_sem=in_recv.at[back, b, part],
            device_id=at(1, dr, dc),
            device_id_type=MESH,
        )

    def extent(section, part):
        cut = half - section
        return (0, cut) if part == 0 else (cut, height)

    def main_copy(b, part, section):
        y0, y1 = extent(section, part)
        span = pl.ds(y0, y1 - y0)
        return pltpu.make_async_remote_copy(
            src_ref=new_hidden.at[b, span],
            dst_ref=main_in.at[b, span],
            send_sem=main_send.at[b, part],
            recv_sem=main_recv.at[b, part],
            device_id=at(1, 0, 0),
            device_id_type=MESH,
        )

    def in_part(d, part):
        dr = AROUND[d][0]
        return dr == 0 or (dr < 0) == (part == 0)

    for b in range(batch):
        for d, (dr, dc) in enumerate(AROUND):

            @pl.when(inside(dr, dc))
            def _():
                own_copy(d, b).start()

            @pl.when(inside(dr, dc) & first)
            def _():
                lat_copy(d, b).start()

    left, right = PAD - 1, PAD + width

    def put_side(dc, y0, y1, strip):
        side = left if dc < 0 else right
        wide[1 + y0 : 1 + y1, side : side + 1, :] = strip.reshape(y1 - y0, 1, chans)

    def put_line(dr, dc, strip):
        y = 0 if dr < 0 else height + 1
        if dc == 0:
            wide[y, PAD : PAD + width, :] = strip
        elif dc < 0:
            wide[y, left : left + 1, :] = strip[width - 1 : width]
        else:
            wide[y, right : right + 1, :] = strip[0:1]

    def put_all(source, halo, b):
        for y in range(height):
            wide[1 + y, PAD : PAD + width, :] = source[b, line(y)].astype(F32)
        for d, (dr, dc) in enumerate(AROUND):
            strip = halo[d, b].astype(F32)
            if dr == 0:
                put_side(dc, 0, height, strip)
            else:
                put_line(dr, dc, strip)

    def convolved(y0, y1, w):
        for dx in range(3):
            taps[y0 : y1 + 2, :, dx * chans : (dx + 1) * chans] = wide[
                y0 : y1 + 2, left + dx : left + dx + width, :
            ].astype(BF16)
        patch = jnp.concatenate(
            [
                taps[y0 + dy : y1 + dy].reshape((y1 - y0) * width, 3 * chans)
                for dy in range(3)
            ],
            axis=-1,
        )
        return jnp.dot(patch, w[...].reshape(9 * chans, -1), preferred_element_type=F32)

    stores = []
    for b in range(batch):
        for d, (dr, dc) in enumerate(AROUND):

            @pl.when(inside(dr, dc))
            def _():
                own_copy(opposite(d), b).wait_recv()

        if b == 0:
            for load in loads[2:5]:
                load.wait()
        put_all(hidden, halo_own, b)
        gates[...] = convolved(0, height, w_own) + bias_ref[...]

        for part in range(2):
            if part == 0:

                @pl.when(first)
                def _():
                    for d, (dr, dc) in enumerate(AROUND):

                        @pl.when(inside(dr, dc))
                        def _():
                            lat_copy(opposite(d), b).wait_recv()

                    put_all(latent, halo_lat, b)

            y0, y1 = (0, half) if part == 0 else (least, height)

            @pl.when(s > 0)
            def _():
                for d, (dr, dc) in enumerate(AROUND):
                    if in_part(d, part):

                        @pl.when(inside(dr, dc))
                        def _():
                            edge_copy(opposite(d), b, part).wait_recv()

                        strip = halo_in[d, b, part].astype(F32)
                        if dr == 0:
                            put_side(dc, y0, y1, strip[: y1 - y0])
                        else:
                            put_line(dr, dc, strip)

            for section in range(1, sections):

                @pl.when(s == section)
                def _():
                    main_copy(b, part, section - 1).wait_recv()
                    m0, m1 = extent(section - 1, part)
                    wide[1 + m0 : 1 + m1, PAD : PAD + width, :] = main_in[b, m0:m1].astype(F32)

            if b == 0 and part == 0:
                for load in loads[5:8]:
                    load.wait()
            z = gates[y0 * width : y1 * width] + convolved(y0, y1, w_in)
            if b == 0 and part == 0:
                loads[8].wait()
            count = (y1 - y0) * width
            old = ordered(cell, b, y0, y1).reshape(count, chans)
            gate_i = sigmoid(z[:, :chans])
            gate_f = sigmoid(z[:, chans : 2 * chans])
            gate_g = jnp.tanh(z[:, 2 * chans : 3 * chans])
            gate_o = sigmoid(z[:, 3 * chans :])
            now = gate_f * old + gate_i * gate_g
            out = (gate_o * jnp.tanh(now)).astype(BF16).reshape(y1 - y0, width, chans)
            now = now.reshape(y1 - y0, width, chans)

            for y in range(y0, y1):
                if part == 0 or y >= half:
                    new_hidden[b, y] = out[y - y0]
                else:

                    @pl.when(y >= half - s)
                    def _():
                        new_hidden[b, y] = out[y - y0]

            tile = out.astype(F32)
            spare = jnp.zeros((height - (y1 - y0), chans), F32)
            for side, x in enumerate((0, width - 1)):
                new_edges[side, b, part] = jnp.concatenate([tile[:, x, :], spare]).astype(BF16)

            if b == 0 and part == 0:

                @pl.when(feeds)
                def _():
                    pl.semaphore_wait(ready, listeners)

            for section in range(sections - 1):

                @pl.when(s == section)
                def _():
                    main_copy(b, part, section).start()

            for d, (dr, dc) in enumerate(AROUND):
                if in_part(d, part):

                    @pl.when(inside(dr, dc) & feeds)
                    def _():
                        edge_copy(d, b, part).start()

            for y in range(y0, y1):
                new_cell[b, line(y)] = now[y - y0]
                out_hidden[b, line(y)] = out[y - y0]

        for k, (src, dst) in enumerate(((new_cell, cell_out), (out_hidden, hidden_out))):
            store = pltpu.make_async_copy(src.at[b], dst.at[0, b], store_sem.at[k, b])
            store.start()
            stores.append(store)

    for b in range(batch):
        for d, (dr, dc) in enumerate(AROUND):

            @pl.when(inside(dr, dc))
            def _():
                own_copy(d, b).wait_send()

            @pl.when(inside(dr, dc) & first)
            def _():
                lat_copy(d, b).wait_send()

            for part in range(2):
                if in_part(d, part):

                    @pl.when(inside(dr, dc) & feeds)
                    def _():
                        edge_copy(d, b, part).wait_send()

        for part in range(2):
            for section in range(sections - 1):

                @pl.when(s == section)
                def _():
                    main_copy(b, part, section).wait_send()

    for store in stores:
        store.wait()


def on_device(latent, hidden_old, cell_old, weights, bias):
    sizes = tuple(lax.axis_size(axis) for axis in ("section", "row", "col"))
    batch, height, width, chans = latent.shape
    gate_chans = weights.shape[-1]
    around = len(AROUND)
    edge = max(height, width)
    assert height == width and height % 16 == 0 and sizes[0] < height // 2
    tile = (batch, height, width, chans)
    dma = pltpu.SemaphoreType.DMA
    anywhere = pl.BlockSpec(memory_space=pltpu.HBM)
    flops = 2 * batch * height * width * 9 * 2 * chans * gate_chans
    return pl.pallas_call(
        functools.partial(kernel, sizes),
        out_shape=(
            jax.ShapeDtypeStruct(hidden_old.shape, BF16),
            jax.ShapeDtypeStruct(cell_old.shape, F32),
        ),
        in_specs=[anywhere] * 4 + [pl.BlockSpec(memory_space=pltpu.VMEM)],
        out_specs=(anywhere, anywhere),
        scratch_shapes=[
            pltpu.VMEM(tile, BF16),
            pltpu.VMEM(tile, BF16),
            pltpu.VMEM(tile, F32),
            pltpu.VMEM((9, chans, gate_chans), BF16),
            pltpu.VMEM((9, chans, gate_chans), BF16),
            pltpu.VMEM(tile, BF16),
            pltpu.VMEM((around, batch, 2, edge, chans), BF16),
            pltpu.VMEM((around, batch, edge, chans), BF16),
            pltpu.VMEM((around, batch, edge, chans), BF16),
            pltpu.VMEM((2, batch, edge, chans), BF16),
            pltpu.VMEM((2, batch, edge, chans), BF16),
            pltpu.VMEM((2, batch, 2, edge, chans), BF16),
            pltpu.VMEM(tile, BF16),
            pltpu.VMEM(tile, BF16),
            pltpu.VMEM(tile, F32),
            pltpu.VMEM((height + 2, width + 2 * PAD, chans), F32),
            pltpu.VMEM((height + 2, width, 3 * chans), BF16),
            pltpu.VMEM((height * width, gate_chans), F32),
            dma((9,)),
            dma((2, batch)),
            dma((around, batch)),
            dma((around, batch)),
            dma((around, batch)),
            dma((around, batch)),
            dma((around, batch, 2)),
            dma((around, batch, 2)),
            dma((batch, 2)),
            dma((batch, 2)),
            pltpu.SemaphoreType.REGULAR,
        ],
        compiler_params=pltpu.CompilerParams(
            collective_id=0, has_side_effects=True, vmem_limit_bytes=64 * 1024 * 1024 - 4096
        ),
        cost_estimate=pl.CostEstimate(
            flops=flops, bytes_accessed=weights.size * 2, transcendentals=0
        ),
    )(latent, hidden_old, cell_old, weights, bias)


def solution(mesh):
    in_specs = (
        P(None, "row", "col", None),
        P("section", None, "row", "col", None),
        P("section", None, "row", "col", None),
        P("section", None, None, None),
        P("section", None),
    )
    out_specs = (P("section", None, "row", "col", None), P("section", None, "row", "col", None))
    return jax.shard_map(
        on_device, mesh=mesh, in_specs=in_specs, out_specs=out_specs, check_vma=False
    )
```

```python
import functools

import jax
import jax.numpy as jnp
from jax import lax
from jax.experimental import pallas as pl
from jax.experimental.pallas import tpu as pltpu
from jax.sharding import PartitionSpec as P

MESH = pl.DeviceIdType.MESH
F32 = jnp.float32
BF16 = jnp.bfloat16
PAD = 8


def directions(sizes):
    across = (-1, 0, 1) if sizes[1] > 2 else (0, 1) if sizes[1] > 1 else (0,)
    along = (-1, 0, 1) if sizes[2] > 1 else (0,)
    return tuple((dr, dc) for dr in across for dc in along if (dr, dc) != (0, 0))


def sigmoid(x):
    return 0.5 * jnp.tanh(0.5 * x) + 0.5


def kernel(
    sizes,
    latent_hbm,
    hidden_hbm,
    cell_hbm,
    weights_hbm,
    bias_ref,
    kept_out,
    added_out,
    opened_out,
    latent,
    hidden,
    cell,
    w_in,
    w_own,
    main_in,
    halo_in,
    corner_in,
    new_corners,
    halo_own,
    halo_lat,
    own_edges,
    lat_edges,
    new_edges,
    new_hidden,
    kept,
    added,
    opened,
    wide,
    taps,
    gates,
    load_sem,
    store_sem,
    own_send,
    own_recv,
    lat_send,
    lat_recv,
    in_recv,
    edge_send,
    main_send,
    main_recv,
    ready,
):
    around = directions(sizes)
    sections, rows, cols = sizes
    batch, height, width, chans = latent.shape
    half = height // 2
    least = half - (sections - 1)
    s = lax.axis_index("section")
    r = lax.axis_index("row")
    c = lax.axis_index("col")
    first = s == 0
    feeds = s + 1 < sections
    odd = lax.rem(r, 2)
    step = 1 - 2 * odd

    def line(y):
        return y + odd * (height - 1 - 2 * y)

    def ordered(source, b, y0, y1):
        return jnp.stack([source[b, line(y)] for y in range(y0, y1)])

    def opposite(d):
        dr, dc = around[d]
        return around.index((dr, -dc))

    def inside(dr, dc):
        return (r + dr * step >= 0) & (r + dr * step < rows) & (c + dc >= 0) & (c + dc < cols)

    def at(ds, dr, dc):
        return (s + ds, r + dr * step, c + dc)

    def taps_of(dy, start):
        return weights_hbm.at[0, pl.ds(3 * (dy + odd * (2 - 2 * dy)), 3), pl.ds(start, chans)]

    loads = [
        pltpu.make_async_copy(src, dst, load_sem.at[k])
        for k, (src, dst) in enumerate(
            [(hidden_hbm.at[0], hidden), (latent_hbm, latent)]
            + [(taps_of(dy, chans), w_own.at[pl.ds(3 * dy, 3)]) for dy in range(3)]
            + [(taps_of(dy, 0), w_in.at[pl.ds(3 * dy, 3)]) for dy in range(3)]
            + [(cell_hbm.at[0], cell)]
        )
    ]
    for load in loads:
        load.start()

    halo_in[...] = jnp.zeros_like(halo_in)
    corner_in[...] = jnp.zeros_like(corner_in)
    halo_own[...] = jnp.zeros_like(halo_own)
    wide[...] = jnp.zeros_like(wide)
    halo_lat[...] = jnp.zeros_like(halo_lat)

    barrier = pltpu.get_barrier_semaphore()
    expected = jnp.int32(0)
    listeners = jnp.int32(0)
    for dr, dc in around + ((0, 0),):
        there = inside(dr, dc)
        if (dr, dc) != (0, 0):

            @pl.when(there)
            def _():
                pl.semaphore_signal(barrier, inc=1, device_id=at(0, dr, dc), device_id_type=MESH)

            expected = expected + there.astype(jnp.int32)

    for dr, dc in around + ((0, 0),):
        there = inside(dr, dc)

        @pl.when(there & feeds)
        def _():
            pl.semaphore_signal(barrier, inc=1, device_id=at(1, dr, dc), device_id_type=MESH)

        expected = expected + (there & (s > 0)).astype(jnp.int32)
        listeners = listeners + (there & feeds).astype(jnp.int32)

    def pack(source, edges, b):
        tile = ordered(source, b, 0, height).astype(F32)
        edges[0, b] = tile[:, 0, :].astype(BF16)
        edges[1, b] = tile[:, width - 1, :].astype(BF16)

    loads[0].wait()
    for b in range(batch):
        pack(hidden, own_edges, b)
    loads[1].wait()

    @pl.when(first)
    def _():
        for b in range(batch):
            pack(latent, lat_edges, b)

    pl.semaphore_wait(barrier, expected)

    for dr, dc in around + ((0, 0),):

        @pl.when(inside(dr, dc) & (s > 0))
        def _():
            pl.semaphore_signal(ready, inc=1, device_id=at(-1, dr, dc), device_id_type=MESH)

    def edge(tile, edges, dr, dc):
        if dr == 0:
            return edges.at[0 if dc < 0 else 1]
        return tile.at[:, line(0 if dr < 0 else height - 1)]

    def own_copy(d):
        dr, dc = around[d]
        back = opposite(d)
        return pltpu.make_async_remote_copy(
            src_ref=edge(hidden, own_edges, dr, dc),
            dst_ref=halo_own.at[back],
            send_sem=own_send.at[d],
            recv_sem=own_recv.at[back],
            device_id=at(0, dr, dc),
            device_id_type=MESH,
        )

    def lat_copy(d):
        dr, dc = around[d]
        back = opposite(d)
        return pltpu.make_async_remote_copy(
            src_ref=edge(latent, lat_edges, dr, dc),
            dst_ref=halo_lat.at[back],
            send_sem=lat_send.at[d],
            recv_sem=lat_recv.at[back],
            device_id=at(0, dr, dc),
            device_id_type=MESH,
        )

    def edge_copy(d, b, part):
        dr, dc = around[d]
        back = opposite(d)
        if dr == 0:
            src, dst = new_edges.at[0 if dc < 0 else 1, b, part], halo_in.at[back, b, part]
        elif dc == 0:
            src, dst = new_hidden.at[b, 0 if dr < 0 else height - 1], halo_in.at[back, b, part]
        else:
            src, dst = new_corners.at[0 if dc < 0 else 1, b, part], corner_in.at[back, b]
        return pltpu.make_async_remote_copy(
            src_ref=src,
            dst_ref=dst,
            send_sem=edge_send.at[d, b, part],
            recv_sem=in_recv.at[back, b, part],
            device_id=at(1, dr, dc),
            device_id_type=MESH,
        )

    def extent(section, part):
        cut = half - section
        return (0, cut) if part == 0 else (cut, height)

    def main_copy(b, part, section):
        y0, y1 = extent(section, part)
        span = pl.ds(y0, y1 - y0)
        return pltpu.make_async_remote_copy(
            src_ref=new_hidden.at[b, span],
            dst_ref=main_in.at[b, span],
            send_sem=main_send.at[b, part],
            recv_sem=main_recv.at[b, part],
            device_id=at(1, 0, 0),
            device_id_type=MESH,
        )

    def in_part(d, part):
        dr = around[d][0]
        return dr == 0 or (dr < 0) == (part == 0)

    for d, (dr, dc) in enumerate(around):

        @pl.when(inside(dr, dc) & first)
        def _():
            lat_copy(d).start()

    for d, (dr, dc) in enumerate(around):

        @pl.when(inside(dr, dc))
        def _():
            own_copy(d).start()

    left, right = PAD - 1, PAD + width

    def put_side(dc, y0, y1, strip):
        side = left if dc < 0 else right
        wide[1 + y0 : 1 + y1, side : side + 1, :] = strip.reshape(y1 - y0, 1, chans)

    def put_line(dr, dc, strip):
        y = 0 if dr < 0 else height + 1
        if dc == 0:
            wide[y, PAD : PAD + width, :] = strip
        elif dc < 0:
            wide[y, left : left + 1, :] = strip[width - 1 : width]
        else:
            wide[y, right : right + 1, :] = strip[0:1]

    def put_all(source, halo, b):
        for y in range(height):
            wide[1 + y, PAD : PAD + width, :] = source[b, line(y)].astype(F32)
        for d, (dr, dc) in enumerate(around):
            strip = halo[d, b].astype(F32)
            if dr == 0:
                put_side(dc, 0, height, strip)
            else:
                put_line(dr, dc, strip)

    def convolved(y0, y1, w):
        for dx in range(3):
            taps[y0 : y1 + 2, :, dx * chans : (dx + 1) * chans] = wide[
                y0 : y1 + 2, left + dx : left + dx + width, :
            ].astype(BF16)
        patch = jnp.concatenate(
            [
                taps[y0 + dy : y1 + dy].reshape((y1 - y0) * width, 3 * chans)
                for dy in range(3)
            ],
            axis=-1,
        )
        return jnp.dot(patch, w[...].reshape(9 * chans, -1), preferred_element_type=F32)

    stores = []
    for b in range(batch):
        if b == 0:
            for d, (dr, dc) in enumerate(around):

                @pl.when(inside(dr, dc))
                def _():
                    own_copy(opposite(d)).wait_recv()

            for load in loads[2:5]:
                load.wait()
        put_all(hidden, halo_own, b)
        gates[...] = convolved(0, height, w_own) + bias_ref[...]

        for part in range(2):
            if part == 0:

                @pl.when(first)
                def _():
                    if b == 0:
                        for d, (dr, dc) in enumerate(around):

                            @pl.when(inside(dr, dc))
                            def _():
                                lat_copy(opposite(d)).wait_recv()

                    put_all(latent, halo_lat, b)

            y0, y1 = (0, half) if part == 0 else (least, height)

            @pl.when(s > 0)
            def _():
                for d, (dr, dc) in enumerate(around):
                    if in_part(d, part):

                        @pl.when(inside(dr, dc))
                        def _():
                            edge_copy(opposite(d), b, part).wait_recv()

                        if dr == 0:
                            strip = halo_in[d, b, part].astype(F32)
                            put_side(dc, y0, y1, strip[: y1 - y0])
                        elif dc == 0:
                            put_line(dr, dc, halo_in[d, b, part].astype(F32))
                        else:
                            y, side = 0 if dr < 0 else height + 1, left if dc < 0 else right
                            wide[y, side : side + 1, :] = corner_in[d, b]

            for section in range(1, sections):

                @pl.when(s == section)
                def _():
                    main_copy(b, part, section - 1).wait_recv()
                    m0, m1 = extent(section - 1, part)
                    wide[1 + m0 : 1 + m1, PAD : PAD + width, :] = main_in[b, m0:m1].astype(F32)

            if b == 0 and part == 0:
                for load in loads[5:8]:
                    load.wait()
            z = gates[y0 * width : y1 * width] + convolved(y0, y1, w_in)
            if b == 0 and part == 0:
                loads[8].wait()
            count = (y1 - y0) * width
            old = ordered(cell, b, y0, y1).reshape(count, chans)
            gate_i = sigmoid(z[:, :chans])
            gate_f = sigmoid(z[:, chans : 2 * chans])
            gate_g = jnp.tanh(z[:, 2 * chans : 3 * chans])
            gate_o = sigmoid(z[:, 3 * chans :])
            keep, add = gate_f * old, gate_i * gate_g
            now = keep + add
            out = (gate_o * jnp.tanh(now)).astype(BF16).reshape(y1 - y0, width, chans)

            for y in range(y0, y1):
                if part == 0 or y >= half:
                    new_hidden[b, y] = out[y - y0]
                else:

                    @pl.when(y >= half - s)
                    def _():
                        new_hidden[b, y] = out[y - y0]

            tile = out.astype(F32)
            spare = jnp.zeros((height - (y1 - y0), chans), F32)
            for side, x in enumerate((0, width - 1)):
                new_edges[side, b, part] = jnp.concatenate([tile[:, x, :], spare]).astype(BF16)
                y = 0 if part == 0 else y1 - y0 - 1
                new_corners[side, b, part] = tile[y, x : x + 1, :]

            if b == 0 and part == 0:

                @pl.when(feeds)
                def _():
                    pl.semaphore_wait(ready, listeners)

            for section in range(sections - 1):

                @pl.when(s == section)
                def _():
                    main_copy(b, part, section).start()

            for d, (dr, dc) in enumerate(around):
                if in_part(d, part):

                    @pl.when(inside(dr, dc) & feeds)
                    def _():
                        edge_copy(d, b, part).start()

            for value, ref in ((keep, kept), (add, added), (gate_o, opened)):
                value = value.reshape(y1 - y0, width, chans)
                for y in range(y0, y1):
                    ref[b, line(y)] = value[y - y0]

        for k, (src, dst) in enumerate(
            ((kept, kept_out), (added, added_out), (opened, opened_out))
        ):
            store = pltpu.make_async_copy(src.at[b], dst.at[0, b], store_sem.at[k, b])
            store.start()
            stores.append(store)

    for d, (dr, dc) in enumerate(around):

        @pl.when(inside(dr, dc))
        def _():
            own_copy(d).wait_send()

        @pl.when(inside(dr, dc) & first)
        def _():
            lat_copy(d).wait_send()

    for b in range(batch):
        for d, (dr, dc) in enumerate(around):
            for part in range(2):
                if in_part(d, part):

                    @pl.when(inside(dr, dc) & feeds)
                    def _():
                        edge_copy(d, b, part).wait_send()

        for part in range(2):
            for section in range(sections - 1):

                @pl.when(s == section)
                def _():
                    main_copy(b, part, section).wait_send()

    for store in stores:
        store.wait()


def on_device(latent, hidden_old, cell_old, weights, bias):
    sizes = tuple(lax.axis_size(axis) for axis in ("section", "row", "col"))
    batch, height, width, chans = latent.shape
    gate_chans = weights.shape[-1]
    around = len(directions(sizes))
    edge = max(height, width)
    assert height == width and height % 16 == 0 and sizes[0] < height // 2
    tile = (batch, height, width, chans)
    dma = pltpu.SemaphoreType.DMA
    anywhere = pl.BlockSpec(memory_space=pltpu.HBM)
    flops = 2 * batch * height * width * 9 * 2 * chans * gate_chans
    kept, added, opened = pl.pallas_call(
        functools.partial(kernel, sizes),
        out_shape=(jax.ShapeDtypeStruct(cell_old.shape, F32),) * 3,
        in_specs=[anywhere] * 4 + [pl.BlockSpec(memory_space=pltpu.VMEM)],
        out_specs=(anywhere,) * 3,
        scratch_shapes=[
            pltpu.VMEM(tile, BF16),
            pltpu.VMEM(tile, BF16),
            pltpu.VMEM(tile, F32),
            pltpu.VMEM((9, chans, gate_chans), BF16),
            pltpu.VMEM((9, chans, gate_chans), BF16),
            pltpu.VMEM(tile, BF16),
            pltpu.VMEM((around, batch, 2, edge, chans), BF16),
            pltpu.VMEM((around, batch, 1, chans), F32),
            pltpu.VMEM((2, batch, 2, 1, chans), F32),
            pltpu.VMEM((around, batch, edge, chans), BF16),
            pltpu.VMEM((around, batch, edge, chans), BF16),
            pltpu.VMEM((2, batch, edge, chans), BF16),
            pltpu.VMEM((2, batch, edge, chans), BF16),
            pltpu.VMEM((2, batch, 2, edge, chans), BF16),
            pltpu.VMEM(tile, BF16),
            pltpu.VMEM(tile, F32),
            pltpu.VMEM(tile, F32),
            pltpu.VMEM(tile, F32),
            pltpu.VMEM((height + 2, width + 2 * PAD, chans), F32),
            pltpu.VMEM((height + 2, width, 3 * chans), BF16),
            pltpu.VMEM((height * width, gate_chans), F32),
            dma((9,)),
            dma((3, batch)),
            dma((around,)),
            dma((around,)),
            dma((around,)),
            dma((around,)),
            dma((around, batch, 2)),
            dma((around, batch, 2)),
            dma((batch, 2)),
            dma((batch, 2)),
            pltpu.SemaphoreType.REGULAR,
        ],
        compiler_params=pltpu.CompilerParams(
            collective_id=0, has_side_effects=True, vmem_limit_bytes=64 * 1024 * 1024 - 4096
        ),
        cost_estimate=pl.CostEstimate(
            flops=flops, bytes_accessed=weights.size * 2, transcendentals=0
        ),
    )(latent, hidden_old, cell_old, weights, bias)
    cell = kept + added
    return (opened * jnp.tanh(cell)).astype(BF16), cell


def solution(mesh):
    in_specs = (
        P(None, "row", "col", None),
        P("section", None, "row", "col", None),
        P("section", None, "row", "col", None),
        P("section", None, None, None),
        P("section", None),
    )
    out_specs = (P("section", None, "row", "col", None), P("section", None, "row", "col", None))
    return jax.shard_map(
        on_device, mesh=mesh, in_specs=in_specs, out_specs=out_specs, check_vma=False
    )
```

```python
import functools

import jax
import jax.numpy as jnp
from jax import lax
from jax.experimental import pallas as pl
from jax.experimental.pallas import tpu as pltpu
from jax.sharding import PartitionSpec as P

MESH = pl.DeviceIdType.MESH
F32 = jnp.float32
BF16 = jnp.bfloat16
PAD = 8


def directions(sizes):
    across = (-1, 0, 1) if sizes[1] > 2 else (0, 1) if sizes[1] > 1 else (0,)
    along = (-1, 0, 1) if sizes[2] > 1 else (0,)
    return tuple((dr, dc) for dr in across for dc in along if (dr, dc) != (0, 0))


def sigmoid(x):
    return 0.5 * jnp.tanh(0.5 * x) + 0.5


def kernel(
    sizes,
    latent_hbm,
    hidden_hbm,
    cell_hbm,
    weights_hbm,
    bias_ref,
    kept_out,
    added_out,
    opened_out,
    latent,
    hidden,
    cell,
    w_in,
    w_own,
    main_in,
    halo_in,
    corner_in,
    new_corners,
    halo_own,
    halo_lat,
    own_edges,
    lat_edges,
    new_edges,
    new_hidden,
    kept,
    added,
    opened,
    wide,
    taps,
    border,
    gates,
    total,
    load_sem,
    store_sem,
    own_send,
    own_recv,
    lat_send,
    lat_recv,
    in_recv,
    edge_send,
    main_send,
    main_recv,
    ready,
):
    around = directions(sizes)
    sections, rows, cols = sizes
    batch, height, width, chans = latent.shape
    half = height // 2
    least = half - (sections - 1)
    s = lax.axis_index("section")
    r = lax.axis_index("row")
    c = lax.axis_index("col")
    first = s == 0
    feeds = s + 1 < sections
    odd = lax.rem(r, 2)
    step = 1 - 2 * odd

    def line(y):
        return y + odd * (height - 1 - 2 * y)

    def ordered(source, b, y0, y1):
        return jnp.stack([source[b, line(y)] for y in range(y0, y1)])

    def opposite(d):
        dr, dc = around[d]
        return around.index((dr, -dc))

    def inside(dr, dc):
        return (r + dr * step >= 0) & (r + dr * step < rows) & (c + dc >= 0) & (c + dc < cols)

    def at(ds, dr, dc):
        return (s + ds, r + dr * step, c + dc)

    def taps_of(dy, start):
        return weights_hbm.at[0, pl.ds(3 * (dy + odd * (2 - 2 * dy)), 3), pl.ds(start, chans)]

    loads = [
        pltpu.make_async_copy(src, dst, load_sem.at[k])
        for k, (src, dst) in enumerate(
            [(hidden_hbm.at[0], hidden), (latent_hbm, latent)]
            + [(taps_of(dy, chans), w_own.at[pl.ds(3 * dy, 3)]) for dy in range(3)]
            + [(taps_of(dy, 0), w_in.at[pl.ds(3 * dy, 3)]) for dy in range(3)]
            + [(cell_hbm.at[0], cell)]
        )
    ]
    for load in loads:
        load.start()

    halo_in[...] = jnp.zeros_like(halo_in)
    corner_in[...] = jnp.zeros_like(corner_in)
    halo_own[...] = jnp.zeros_like(halo_own)
    wide[...] = jnp.zeros_like(wide)
    halo_lat[...] = jnp.zeros_like(halo_lat)

    barrier = pltpu.get_barrier_semaphore()
    expected = jnp.int32(0)
    listeners = jnp.int32(0)
    for dr, dc in around + ((0, 0),):
        there = inside(dr, dc)
        if (dr, dc) != (0, 0):

            @pl.when(there)
            def _():
                pl.semaphore_signal(barrier, inc=1, device_id=at(0, dr, dc), device_id_type=MESH)

            expected = expected + there.astype(jnp.int32)

    for dr, dc in around + ((0, 0),):
        there = inside(dr, dc)

        @pl.when(there & feeds)
        def _():
            pl.semaphore_signal(barrier, inc=1, device_id=at(1, dr, dc), device_id_type=MESH)

        expected = expected + (there & (s > 0)).astype(jnp.int32)
        listeners = listeners + (there & feeds).astype(jnp.int32)

    def pack(source, edges, b):
        tile = ordered(source, b, 0, height).astype(F32)
        edges[0, b] = tile[:, 0, :].astype(BF16)
        edges[1, b] = tile[:, width - 1, :].astype(BF16)

    loads[0].wait()
    for b in range(batch):
        pack(hidden, own_edges, b)
    loads[1].wait()

    @pl.when(first)
    def _():
        for b in range(batch):
            pack(latent, lat_edges, b)

    pl.semaphore_wait(barrier, expected)

    for dr, dc in around + ((0, 0),):

        @pl.when(inside(dr, dc) & (s > 0))
        def _():
            pl.semaphore_signal(ready, inc=1, device_id=at(-1, dr, dc), device_id_type=MESH)

    def edge(tile, edges, dr, dc):
        if dr == 0:
            return edges.at[0 if dc < 0 else 1]
        return tile.at[:, line(0 if dr < 0 else height - 1)]

    def own_copy(d):
        dr, dc = around[d]
        back = opposite(d)
        return pltpu.make_async_remote_copy(
            src_ref=edge(hidden, own_edges, dr, dc),
            dst_ref=halo_own.at[back],
            send_sem=own_send.at[d],
            recv_sem=own_recv.at[back],
            device_id=at(0, dr, dc),
            device_id_type=MESH,
        )

    def lat_copy(d):
        dr, dc = around[d]
        back = opposite(d)
        return pltpu.make_async_remote_copy(
            src_ref=edge(latent, lat_edges, dr, dc),
            dst_ref=halo_lat.at[back],
            send_sem=lat_send.at[d],
            recv_sem=lat_recv.at[back],
            device_id=at(0, dr, dc),
            device_id_type=MESH,
        )

    def edge_copy(d, b, part):
        dr, dc = around[d]
        back = opposite(d)
        if dr == 0:
            src, dst = new_edges.at[0 if dc < 0 else 1, b, part], halo_in.at[back, b, part]
        elif dc == 0:
            src, dst = new_hidden.at[b, 0 if dr < 0 else height - 1], halo_in.at[back, b, part]
        else:
            src, dst = new_corners.at[0 if dc < 0 else 1, b, part], corner_in.at[back, b]
        return pltpu.make_async_remote_copy(
            src_ref=src,
            dst_ref=dst,
            send_sem=edge_send.at[d, b, part],
            recv_sem=in_recv.at[back, b, part],
            device_id=at(1, dr, dc),
            device_id_type=MESH,
        )

    def extent(section, part):
        cut = half - section
        return (0, cut) if part == 0 else (cut, height)

    def main_copy(b, part, section):
        y0, y1 = extent(section, part)
        span = pl.ds(y0, y1 - y0)
        return pltpu.make_async_remote_copy(
            src_ref=new_hidden.at[b, span],
            dst_ref=main_in.at[b, span],
            send_sem=main_send.at[b, part],
            recv_sem=main_recv.at[b, part],
            device_id=at(1, 0, 0),
            device_id_type=MESH,
        )

    def in_part(d, part):
        dr = around[d][0]
        return dr == 0 or (dr < 0) == (part == 0)

    for d, (dr, dc) in enumerate(around):

        @pl.when(inside(dr, dc) & first)
        def _():
            lat_copy(d).start()

    for d, (dr, dc) in enumerate(around):

        @pl.when(inside(dr, dc))
        def _():
            own_copy(d).start()

    left, right = PAD - 1, PAD + width

    def put_side(dc, y0, y1, strip):
        side = left if dc < 0 else right
        wide[1 + y0 : 1 + y1, side : side + 1, :] = strip.reshape(y1 - y0, 1, chans)

    def put_line(dr, strip):
        wide[0 if dr < 0 else height + 1, PAD : PAD + width, :] = strip

    def put_tile(source, b):
        for y in range(height):
            wide[1 + y, PAD : PAD + width, :] = source[b, line(y)].astype(F32)

    def convolved(y0, y1, w):
        for dx in range(3):
            taps[y0 : y1 + 2, :, dx * chans : (dx + 1) * chans] = wide[
                y0 : y1 + 2, left + dx : left + dx + width, :
            ].astype(BF16)
        patch = jnp.concatenate(
            [
                taps[y0 + dy : y1 + dy].reshape((y1 - y0) * width, 3 * chans)
                for dy in range(3)
            ],
            axis=-1,
        )
        return jnp.dot(patch, w[...].reshape(9 * chans, -1), preferred_element_type=F32)

    def add_borders(halo, w):
        side_cells = height
        for d, (dr, dc) in enumerate(around):
            if dr != 0 and dc != 0:
                continue
            border[:, PAD : PAD + side_cells, :] = halo[d].astype(F32)
            for end, place in ((-1, PAD - 1), (1, PAD + side_cells)):
                if dr == 0 and (end, dc) in around:
                    x = width - 1 if dc < 0 else 0
                    corner = halo[around.index((end, dc))].astype(F32)[:, x : x + 1, :]
                else:
                    corner = jnp.zeros((batch, 1, chans), F32)
                border[:, place : place + 1, :] = corner
            patch = jnp.concatenate(
                [
                    border[:, PAD - 1 + k : PAD - 1 + k + side_cells, :].reshape(-1, chans)
                    for k in range(3)
                ],
                axis=-1,
            ).astype(BF16)
            if dr == 0:
                part_w = jnp.concatenate([w[3 * k + 1 + dc] for k in range(3)], axis=0)
            else:
                part_w = w[3 + 3 * dr : 6 + 3 * dr].reshape(3 * chans, -1)
            more = jnp.dot(patch, part_w, preferred_element_type=F32)
            more = more.reshape(batch, side_cells, -1)
            if dr == 0:
                x = 0 if dc < 0 else width - 1
                for b in range(batch):
                    gates[b, :, x, :] += more[b]
            else:
                gates[:, 0 if dr < 0 else height - 1] += more

    for load in loads[2:5]:
        load.wait()
    for b in range(batch):
        put_tile(hidden, b)
        gates[b] = (convolved(0, height, w_own) + bias_ref[...]).reshape(height, width, -1)
    for load in loads[5:8]:
        load.wait()

    @pl.when(first)
    def _():
        for b in range(batch):
            put_tile(latent, b)
            gates[b] += convolved(0, height, w_in).reshape(height, width, -1)

        for d, (dr, dc) in enumerate(around):

            @pl.when(inside(dr, dc))
            def _():
                lat_copy(opposite(d)).wait_recv()

        add_borders(halo_lat, w_in)

    for d, (dr, dc) in enumerate(around):

        @pl.when(inside(dr, dc))
        def _():
            own_copy(opposite(d)).wait_recv()

    add_borders(halo_own, w_own)
    loads[8].wait()

    stores = []
    for b in range(batch):
        for part in range(2):
            y0, y1 = (0, half) if part == 0 else (least, height)

            @pl.when(s > 0)
            def _():
                for d, (dr, dc) in enumerate(around):
                    if in_part(d, part):

                        @pl.when(inside(dr, dc))
                        def _():
                            edge_copy(opposite(d), b, part).wait_recv()

                        if dr == 0:
                            strip = halo_in[d, b, part].astype(F32)
                            put_side(dc, y0, y1, strip[: y1 - y0])
                        elif dc == 0:
                            put_line(dr, halo_in[d, b, part].astype(F32))
                        else:
                            y, side = 0 if dr < 0 else height + 1, left if dc < 0 else right
                            wide[y, side : side + 1, :] = corner_in[d, b]

            for section in range(1, sections):

                @pl.when(s == section)
                def _():
                    main_copy(b, part, section - 1).wait_recv()
                    m0, m1 = extent(section - 1, part)
                    wide[1 + m0 : 1 + m1, PAD : PAD + width, :] = main_in[b, m0:m1].astype(F32)

            count = (y1 - y0) * width

            @pl.when(first)
            def _():
                total[:count] = gates[b, y0:y1].reshape(count, -1)

            @pl.when(s > 0)
            def _():
                total[:count] = gates[b, y0:y1].reshape(count, -1) + convolved(y0, y1, w_in)

            z = total[:count]
            old = ordered(cell, b, y0, y1).reshape(count, chans)
            gate_i = sigmoid(z[:, :chans])
            gate_f = sigmoid(z[:, chans : 2 * chans])
            gate_g = jnp.tanh(z[:, 2 * chans : 3 * chans])
            gate_o = sigmoid(z[:, 3 * chans :])
            keep, add = gate_f * old, gate_i * gate_g
            now = keep + add
            out = (gate_o * jnp.tanh(now)).astype(BF16).reshape(y1 - y0, width, chans)

            for y in range(y0, y1):
                if part == 0 or y >= half:
                    new_hidden[b, y] = out[y - y0]
                else:

                    @pl.when(y >= half - s)
                    def _():
                        new_hidden[b, y] = out[y - y0]

            tile = out.astype(F32)
            spare = jnp.zeros((height - (y1 - y0), chans), F32)
            for side, x in enumerate((0, width - 1)):
                new_edges[side, b, part] = jnp.concatenate([tile[:, x, :], spare]).astype(BF16)
                y = 0 if part == 0 else y1 - y0 - 1
                new_corners[side, b, part] = tile[y, x : x + 1, :]

            if b == 0 and part == 0:

                @pl.when(feeds)
                def _():
                    pl.semaphore_wait(ready, listeners)

            for section in range(sections - 1):

                @pl.when(s == section)
                def _():
                    main_copy(b, part, section).start()

            for d, (dr, dc) in enumerate(around):
                if in_part(d, part):

                    @pl.when(inside(dr, dc) & feeds)
                    def _():
                        edge_copy(d, b, part).start()

            for value, ref in ((keep, kept), (add, added), (gate_o, opened)):
                value = value.reshape(y1 - y0, width, chans)
                for y in range(y0, y1):
                    ref[b, line(y)] = value[y - y0]

        for k, (src, dst) in enumerate(
            ((kept, kept_out), (added, added_out), (opened, opened_out))
        ):
            store = pltpu.make_async_copy(src.at[b], dst.at[0, b], store_sem.at[k, b])
            store.start()
            stores.append(store)

    for d, (dr, dc) in enumerate(around):

        @pl.when(inside(dr, dc))
        def _():
            own_copy(d).wait_send()

        @pl.when(inside(dr, dc) & first)
        def _():
            lat_copy(d).wait_send()

    for b in range(batch):
        for d, (dr, dc) in enumerate(around):
            for part in range(2):
                if in_part(d, part):

                    @pl.when(inside(dr, dc) & feeds)
                    def _():
                        edge_copy(d, b, part).wait_send()

        for part in range(2):
            for section in range(sections - 1):

                @pl.when(s == section)
                def _():
                    main_copy(b, part, section).wait_send()

    for store in stores:
        store.wait()


def on_device(latent, hidden_old, cell_old, weights, bias):
    sizes = tuple(lax.axis_size(axis) for axis in ("section", "row", "col"))
    batch, height, width, chans = latent.shape
    gate_chans = weights.shape[-1]
    around = len(directions(sizes))
    edge = max(height, width)
    assert height == width and height % 16 == 0 and sizes[0] < height // 2
    tile = (batch, height, width, chans)
    dma = pltpu.SemaphoreType.DMA
    anywhere = pl.BlockSpec(memory_space=pltpu.HBM)
    flops = 2 * batch * height * width * 9 * 2 * chans * gate_chans
    kept, added, opened = pl.pallas_call(
        functools.partial(kernel, sizes),
        out_shape=(jax.ShapeDtypeStruct(cell_old.shape, F32),) * 3,
        in_specs=[anywhere] * 4 + [pl.BlockSpec(memory_space=pltpu.VMEM)],
        out_specs=(anywhere,) * 3,
        scratch_shapes=[
            pltpu.VMEM(tile, BF16),
            pltpu.VMEM(tile, BF16),
            pltpu.VMEM(tile, F32),
            pltpu.VMEM((9, chans, gate_chans), BF16),
            pltpu.VMEM((9, chans, gate_chans), BF16),
            pltpu.VMEM(tile, BF16),
            pltpu.VMEM((around, batch, 2, edge, chans), BF16),
            pltpu.VMEM((around, batch, 1, chans), F32),
            pltpu.VMEM((2, batch, 2, 1, chans), F32),
            pltpu.VMEM((around, batch, edge, chans), BF16),
            pltpu.VMEM((around, batch, edge, chans), BF16),
            pltpu.VMEM((2, batch, edge, chans), BF16),
            pltpu.VMEM((2, batch, edge, chans), BF16),
            pltpu.VMEM((2, batch, 2, edge, chans), BF16),
            pltpu.VMEM(tile, BF16),
            pltpu.VMEM(tile, F32),
            pltpu.VMEM(tile, F32),
            pltpu.VMEM(tile, F32),
            pltpu.VMEM((height + 2, width + 2 * PAD, chans), F32),
            pltpu.VMEM((height + 2, width, 3 * chans), BF16),
            pltpu.VMEM((batch, edge + 2 * PAD, chans), F32),
            pltpu.VMEM((batch, height, width, gate_chans), F32),
            pltpu.VMEM((height * width, gate_chans), F32),
            dma((9,)),
            dma((3, batch)),
            dma((around,)),
            dma((around,)),
            dma((around,)),
            dma((around,)),
            dma((around, batch, 2)),
            dma((around, batch, 2)),
            dma((batch, 2)),
            dma((batch, 2)),
            pltpu.SemaphoreType.REGULAR,
        ],
        compiler_params=pltpu.CompilerParams(
            collective_id=0, has_side_effects=True, vmem_limit_bytes=64 * 1024 * 1024 - 4096
        ),
        cost_estimate=pl.CostEstimate(
            flops=flops, bytes_accessed=weights.size * 2, transcendentals=0
        ),
    )(latent, hidden_old, cell_old, weights, bias)
    cell = kept + added
    return (opened * jnp.tanh(cell)).astype(BF16), cell


def solution(mesh):
    in_specs = (
        P(None, "row", "col", None),
        P("section", None, "row", "col", None),
        P("section", None, "row", "col", None),
        P("section", None, None, None),
        P("section", None),
    )
    out_specs = (P("section", None, "row", "col", None), P("section", None, "row", "col", None))
    return jax.shard_map(
        on_device, mesh=mesh, in_specs=in_specs, out_specs=out_specs, check_vma=False
    )
```

```python
import functools

import jax
import jax.numpy as jnp
from jax import lax
from jax.experimental import pallas as pl
from jax.experimental.pallas import tpu as pltpu
from jax.sharding import PartitionSpec as P

MESH = pl.DeviceIdType.MESH
F32 = jnp.float32
BF16 = jnp.bfloat16
PAD = 8


def directions(sizes):
    across = (-1, 0, 1) if sizes[1] > 2 else (0, 1) if sizes[1] > 1 else (0,)
    along = (-1, 0, 1) if sizes[2] > 1 else (0,)
    return tuple((dr, dc) for dr in across for dc in along if (dr, dc) != (0, 0))


def sigmoid(x):
    return 0.5 * jnp.tanh(0.5 * x) + 0.5


def kernel(
    sizes,
    latent_hbm,
    hidden_hbm,
    cell_hbm,
    weights_hbm,
    bias_ref,
    kept_out,
    added_out,
    opened_out,
    latent,
    hidden,
    cell,
    w_in,
    w_own,
    main_in,
    halo_in,
    corner_in,
    new_corners,
    halo_own,
    halo_lat,
    own_edges,
    lat_edges,
    new_edges,
    new_hidden,
    kept,
    added,
    opened,
    wide,
    taps,
    border,
    gates,
    total,
    load_sem,
    store_sem,
    own_send,
    own_recv,
    lat_send,
    lat_recv,
    in_recv,
    edge_send,
    main_send,
    main_recv,
    ready,
):
    around = directions(sizes)
    sections, rows, cols = sizes
    batch, height, width, chans = latent.shape
    half = height * 5 // 8
    least = half - (sections - 1)
    s = lax.axis_index("section")
    r = lax.axis_index("row")
    c = lax.axis_index("col")
    first = s == 0
    feeds = s + 1 < sections
    odd = lax.rem(r, 2)
    step = 1 - 2 * odd

    def line(y):
        return y + odd * (height - 1 - 2 * y)

    def ordered(source, b, y0, y1):
        return jnp.stack([source[b, line(y)] for y in range(y0, y1)])

    def opposite(d):
        dr, dc = around[d]
        return around.index((dr, -dc))

    def inside(dr, dc):
        return (r + dr * step >= 0) & (r + dr * step < rows) & (c + dc >= 0) & (c + dc < cols)

    def at(ds, dr, dc):
        return (s + ds, r + dr * step, c + dc)

    def taps_of(dy, start):
        return weights_hbm.at[0, pl.ds(3 * (dy + odd * (2 - 2 * dy)), 3), pl.ds(start, chans)]

    loads = [
        pltpu.make_async_copy(src, dst, load_sem.at[k])
        for k, (src, dst) in enumerate(
            [(hidden_hbm.at[0], hidden), (latent_hbm, latent)]
            + [(taps_of(dy, chans), w_own.at[pl.ds(3 * dy, 3)]) for dy in range(3)]
            + [(taps_of(dy, 0), w_in.at[pl.ds(3 * dy, 3)]) for dy in range(3)]
            + [(cell_hbm.at[0], cell)]
        )
    ]
    for load in loads[:2]:
        load.start()

    halo_in[...] = jnp.zeros_like(halo_in)
    corner_in[...] = jnp.zeros_like(corner_in)
    halo_own[...] = jnp.zeros_like(halo_own)
    wide[...] = jnp.zeros_like(wide)
    halo_lat[...] = jnp.zeros_like(halo_lat)

    barrier = pltpu.get_barrier_semaphore()
    expected = jnp.int32(0)
    listeners = jnp.int32(0)
    for dr, dc in around + ((0, 0),):
        there = inside(dr, dc)
        if (dr, dc) != (0, 0):

            @pl.when(there)
            def _():
                pl.semaphore_signal(barrier, inc=1, device_id=at(0, dr, dc), device_id_type=MESH)

            expected = expected + there.astype(jnp.int32)

    for dr, dc in around + ((0, 0),):
        there = inside(dr, dc)

        @pl.when(there & feeds)
        def _():
            pl.semaphore_signal(barrier, inc=1, device_id=at(1, dr, dc), device_id_type=MESH)

        expected = expected + (there & (s > 0)).astype(jnp.int32)
        listeners = listeners + (there & feeds).astype(jnp.int32)

    for load in loads[2:]:
        load.start()

    def pack(source, edges, b):
        tile = ordered(source, b, 0, height).astype(F32)
        edges[0, b] = tile[:, 0, :].astype(BF16)
        edges[1, b] = tile[:, width - 1, :].astype(BF16)

    loads[0].wait()
    for b in range(batch):
        pack(hidden, own_edges, b)
    loads[1].wait()

    @pl.when(first)
    def _():
        for b in range(batch):
            pack(latent, lat_edges, b)

    pl.semaphore_wait(barrier, expected)

    for dr, dc in around + ((0, 0),):

        @pl.when(inside(dr, dc) & (s > 0))
        def _():
            pl.semaphore_signal(ready, inc=1, device_id=at(-1, dr, dc), device_id_type=MESH)

    def edge(tile, edges, dr, dc):
        if dr == 0:
            return edges.at[0 if dc < 0 else 1]
        return tile.at[:, line(0 if dr < 0 else height - 1)]

    def own_copy(d):
        dr, dc = around[d]
        back = opposite(d)
        return pltpu.make_async_remote_copy(
            src_ref=edge(hidden, own_edges, dr, dc),
            dst_ref=halo_own.at[back],
            send_sem=own_send.at[d],
            recv_sem=own_recv.at[back],
            device_id=at(0, dr, dc),
            device_id_type=MESH,
        )

    def lat_copy(d):
        dr, dc = around[d]
        back = opposite(d)
        return pltpu.make_async_remote_copy(
            src_ref=edge(latent, lat_edges, dr, dc),
            dst_ref=halo_lat.at[back],
            send_sem=lat_send.at[d],
            recv_sem=lat_recv.at[back],
            device_id=at(0, dr, dc),
            device_id_type=MESH,
        )

    def edge_copy(d, b, part):
        dr, dc = around[d]
        back = opposite(d)
        if dr == 0:
            src, dst = new_edges.at[0 if dc < 0 else 1, b, part], halo_in.at[back, b, part]
        elif dc == 0:
            src, dst = new_hidden.at[b, 0 if dr < 0 else height - 1], halo_in.at[back, b, part]
        else:
            src, dst = new_corners.at[0 if dc < 0 else 1, b, part], corner_in.at[back, b]
        return pltpu.make_async_remote_copy(
            src_ref=src,
            dst_ref=dst,
            send_sem=edge_send.at[d, b, part],
            recv_sem=in_recv.at[back, b, part],
            device_id=at(1, dr, dc),
            device_id_type=MESH,
        )

    def extent(section, part):
        cut = half - section
        return (0, cut) if part == 0 else (cut, height)

    def main_copy(b, part, section):
        y0, y1 = extent(section, part)
        span = pl.ds(y0, y1 - y0)
        return pltpu.make_async_remote_copy(
            src_ref=new_hidden.at[b, span],
            dst_ref=main_in.at[b, span],
            send_sem=main_send.at[b, part],
            recv_sem=main_recv.at[b, part],
            device_id=at(1, 0, 0),
            device_id_type=MESH,
        )

    def in_part(d, part):
        dr = around[d][0]
        return dr == 0 or (dr < 0) == (part == 0)

    for d, (dr, dc) in enumerate(around):

        @pl.when(inside(dr, dc) & first)
        def _():
            lat_copy(d).start()

    for d, (dr, dc) in enumerate(around):

        @pl.when(inside(dr, dc))
        def _():
            own_copy(d).start()

    left, right = PAD - 1, PAD + width

    def put_side(dc, y0, y1, strip):
        side = left if dc < 0 else right
        wide[1 + y0 : 1 + y1, side : side + 1, :] = strip.reshape(y1 - y0, 1, chans)

    def put_line(dr, strip):
        wide[0 if dr < 0 else height + 1, PAD : PAD + width, :] = strip

    def put_tile(source, b):
        for y in range(height):
            wide[1 + y, PAD : PAD + width, :] = source[b, line(y)].astype(F32)

    def convolved(y0, y1, w):
        for dx in range(3):
            taps[y0 : y1 + 2, :, dx * chans : (dx + 1) * chans] = wide[
                y0 : y1 + 2, left + dx : left + dx + width, :
            ].astype(BF16)
        patch = jnp.concatenate(
            [
                taps[y0 + dy : y1 + dy].reshape((y1 - y0) * width, 3 * chans)
                for dy in range(3)
            ],
            axis=-1,
        )
        return jnp.dot(patch, w[...].reshape(9 * chans, -1), preferred_element_type=F32)

    def add_borders(halo, w):
        side_cells = height
        for d, (dr, dc) in enumerate(around):
            if dr != 0 and dc != 0:
                continue
            border[:, PAD : PAD + side_cells, :] = halo[d].astype(F32)
            for end, place in ((-1, PAD - 1), (1, PAD + side_cells)):
                if dr == 0 and (end, dc) in around:
                    x = width - 1 if dc < 0 else 0
                    corner = halo[around.index((end, dc))].astype(F32)[:, x : x + 1, :]
                else:
                    corner = jnp.zeros((batch, 1, chans), F32)
                border[:, place : place + 1, :] = corner
            patch = jnp.concatenate(
                [
                    border[:, PAD - 1 + k : PAD - 1 + k + side_cells, :].reshape(-1, chans)
                    for k in range(3)
                ],
                axis=-1,
            ).astype(BF16)
            if dr == 0:
                part_w = jnp.concatenate([w[3 * k + 1 + dc] for k in range(3)], axis=0)
            else:
                part_w = w[3 + 3 * dr : 6 + 3 * dr].reshape(3 * chans, -1)
            more = jnp.dot(patch, part_w, preferred_element_type=F32)
            more = more.reshape(batch, side_cells, -1)
            if dr == 0:
                x = 0 if dc < 0 else width - 1
                for b in range(batch):
                    gates[b, :, x, :] += more[b]
            else:
                gates[:, 0 if dr < 0 else height - 1] += more

    for load in loads[2:5]:
        load.wait()
    for b in range(batch):
        put_tile(hidden, b)
        gates[b] = (convolved(0, height, w_own) + bias_ref[...]).reshape(height, width, -1)
    for load in loads[5:8]:
        load.wait()

    @pl.when(first)
    def _():
        for b in range(batch):
            put_tile(latent, b)
            gates[b] += convolved(0, height, w_in).reshape(height, width, -1)

        for d, (dr, dc) in enumerate(around):

            @pl.when(inside(dr, dc))
            def _():
                lat_copy(opposite(d)).wait_recv()

        add_borders(halo_lat, w_in)

    for d, (dr, dc) in enumerate(around):

        @pl.when(inside(dr, dc))
        def _():
            own_copy(opposite(d)).wait_recv()

    add_borders(halo_own, w_own)
    loads[8].wait()

    stores = []
    for b in range(batch):
        for part in range(2):
            y0, y1 = (0, half) if part == 0 else (least, height)

            @pl.when(s > 0)
            def _():
                for d, (dr, dc) in enumerate(around):
                    if in_part(d, part):

                        @pl.when(inside(dr, dc))
                        def _():
                            edge_copy(opposite(d), b, part).wait_recv()

                        if dr == 0:
                            strip = halo_in[d, b, part].astype(F32)
                            put_side(dc, y0, y1, strip[: y1 - y0])
                        elif dc == 0:
                            put_line(dr, halo_in[d, b, part].astype(F32))
                        else:
                            y, side = 0 if dr < 0 else height + 1, left if dc < 0 else right
                            wide[y, side : side + 1, :] = corner_in[d, b]

            for section in range(1, sections):

                @pl.when(s == section)
                def _():
                    main_copy(b, part, section - 1).wait_recv()
                    m0, m1 = extent(section - 1, part)
                    wide[1 + m0 : 1 + m1, PAD : PAD + width, :] = main_in[b, m0:m1].astype(F32)

            count = (y1 - y0) * width

            @pl.when(first)
            def _():
                total[:count] = gates[b, y0:y1].reshape(count, -1)

            @pl.when(s > 0)
            def _():
                total[:count] = gates[b, y0:y1].reshape(count, -1) + convolved(y0, y1, w_in)

            z = total[:count]
            old = ordered(cell, b, y0, y1).reshape(count, chans)
            gate_i = sigmoid(z[:, :chans])
            gate_f = sigmoid(z[:, chans : 2 * chans])
            gate_g = jnp.tanh(z[:, 2 * chans : 3 * chans])
            gate_o = sigmoid(z[:, 3 * chans :])
            keep, add = gate_f * old, gate_i * gate_g
            now = keep + add
            out = (gate_o * jnp.tanh(now)).astype(BF16).reshape(y1 - y0, width, chans)

            for y in range(y0, y1):
                if part == 0 or y >= half:
                    new_hidden[b, y] = out[y - y0]
                else:

                    @pl.when(y >= half - s)
                    def _():
                        new_hidden[b, y] = out[y - y0]

            tile = out.astype(F32)
            spare = jnp.zeros((height - (y1 - y0), chans), F32)
            for side, x in enumerate((0, width - 1)):
                new_edges[side, b, part] = jnp.concatenate([tile[:, x, :], spare]).astype(BF16)
                y = 0 if part == 0 else y1 - y0 - 1
                new_corners[side, b, part] = tile[y, x : x + 1, :]

            if b == 0 and part == 0:

                @pl.when(feeds)
                def _():
                    pl.semaphore_wait(ready, listeners)

            for d, (dr, dc) in enumerate(around):
                if in_part(d, part):

                    @pl.when(inside(dr, dc) & feeds)
                    def _():
                        edge_copy(d, b, part).start()

            for section in range(sections - 1):

                @pl.when(s == section)
                def _():
                    main_copy(b, part, section).start()

            for value, ref in ((keep, kept), (add, added), (gate_o, opened)):
                value = value.reshape(y1 - y0, width, chans)
                for y in range(y0, y1):
                    ref[b, line(y)] = value[y - y0]

        for k, (src, dst) in enumerate(
            ((kept, kept_out), (added, added_out), (opened, opened_out))
        ):
            store = pltpu.make_async_copy(src.at[b], dst.at[0, b], store_sem.at[k, b])
            store.start()
            stores.append(store)

    for d, (dr, dc) in enumerate(around):

        @pl.when(inside(dr, dc))
        def _():
            own_copy(d).wait_send()

        @pl.when(inside(dr, dc) & first)
        def _():
            lat_copy(d).wait_send()

    for b in range(batch):
        for d, (dr, dc) in enumerate(around):
            for part in range(2):
                if in_part(d, part):

                    @pl.when(inside(dr, dc) & feeds)
                    def _():
                        edge_copy(d, b, part).wait_send()

        for part in range(2):
            for section in range(sections - 1):

                @pl.when(s == section)
                def _():
                    main_copy(b, part, section).wait_send()

    for store in stores:
        store.wait()


def on_device(latent, hidden_old, cell_old, weights, bias):
    sizes = tuple(lax.axis_size(axis) for axis in ("section", "row", "col"))
    batch, height, width, chans = latent.shape
    gate_chans = weights.shape[-1]
    around = len(directions(sizes))
    edge = max(height, width)
    assert height == width and height % 16 == 0 and sizes[0] < height // 2
    tile = (batch, height, width, chans)
    dma = pltpu.SemaphoreType.DMA
    anywhere = pl.BlockSpec(memory_space=pltpu.HBM)
    flops = 2 * batch * height * width * 9 * 2 * chans * gate_chans
    kept, added, opened = pl.pallas_call(
        functools.partial(kernel, sizes),
        out_shape=(jax.ShapeDtypeStruct(cell_old.shape, F32),) * 3,
        in_specs=[anywhere] * 4 + [pl.BlockSpec(memory_space=pltpu.VMEM)],
        out_specs=(anywhere,) * 3,
        scratch_shapes=[
            pltpu.VMEM(tile, BF16),
            pltpu.VMEM(tile, BF16),
            pltpu.VMEM(tile, F32),
            pltpu.VMEM((9, chans, gate_chans), BF16),
            pltpu.VMEM((9, chans, gate_chans), BF16),
            pltpu.VMEM(tile, BF16),
            pltpu.VMEM((around, batch, 2, edge, chans), BF16),
            pltpu.VMEM((around, batch, 1, chans), F32),
            pltpu.VMEM((2, batch, 2, 1, chans), F32),
            pltpu.VMEM((around, batch, edge, chans), BF16),
            pltpu.VMEM((around, batch, edge, chans), BF16),
            pltpu.VMEM((2, batch, edge, chans), BF16),
            pltpu.VMEM((2, batch, edge, chans), BF16),
            pltpu.VMEM((2, batch, 2, edge, chans), BF16),
            pltpu.VMEM(tile, BF16),
            pltpu.VMEM(tile, F32),
            pltpu.VMEM(tile, F32),
            pltpu.VMEM(tile, F32),
            pltpu.VMEM((height + 2, width + 2 * PAD, chans), F32),
            pltpu.VMEM((height + 2, width, 3 * chans), BF16),
            pltpu.VMEM((batch, edge + 2 * PAD, chans), F32),
            pltpu.VMEM((batch, height, width, gate_chans), F32),
            pltpu.VMEM((height * width, gate_chans), F32),
            dma((9,)),
            dma((3, batch)),
            dma((around,)),
            dma((around,)),
            dma((around,)),
            dma((around,)),
            dma((around, batch, 2)),
            dma((around, batch, 2)),
            dma((batch, 2)),
            dma((batch, 2)),
            pltpu.SemaphoreType.REGULAR,
        ],
        compiler_params=pltpu.CompilerParams(
            collective_id=0, has_side_effects=True, vmem_limit_bytes=64 * 1024 * 1024 - 4096
        ),
        cost_estimate=pl.CostEstimate(
            flops=flops, bytes_accessed=weights.size * 2, transcendentals=0
        ),
    )(latent, hidden_old, cell_old, weights, bias)
    cell = kept + added
    return (opened * jnp.tanh(cell)).astype(BF16), cell


def solution(mesh):
    in_specs = (
        P(None, "row", "col", None),
        P("section", None, "row", "col", None),
        P("section", None, "row", "col", None),
        P("section", None, None, None),
        P("section", None),
    )
    out_specs = (P("section", None, "row", "col", None), P("section", None, "row", "col", None))
    return jax.shard_map(
        on_device, mesh=mesh, in_specs=in_specs, out_specs=out_specs, check_vma=False
    )
```

```python
import functools

import jax
import jax.numpy as jnp
from jax import lax
from jax.experimental import pallas as pl
from jax.experimental.pallas import tpu as pltpu
from jax.sharding import PartitionSpec as P

MESH = pl.DeviceIdType.MESH
F32 = jnp.float32
BF16 = jnp.bfloat16
PAD = 8


def directions(sizes):
    across = (-1, 0, 1) if sizes[1] > 2 else (0, 1) if sizes[1] > 1 else (0,)
    along = (-1, 0, 1) if sizes[2] > 1 else (0,)
    return tuple((dr, dc) for dr in across for dc in along if (dr, dc) != (0, 0))


def sigmoid(x):
    return 0.5 * jnp.tanh(0.5 * x) + 0.5


def kernel(
    sizes,
    latent_hbm,
    hidden_hbm,
    cell_hbm,
    weights_hbm,
    bias_ref,
    kept_out,
    added_out,
    opened_out,
    latent,
    hidden,
    cell,
    w_in,
    w_own,
    main_in,
    passing,
    halo_in,
    corner_in,
    new_corners,
    halo_own,
    halo_lat,
    own_edges,
    lat_edges,
    new_edges,
    new_hidden,
    kept,
    added,
    opened,
    wide,
    taps,
    border,
    gates,
    total,
    load_sem,
    store_sem,
    own_send,
    own_recv,
    lat_send,
    lat_recv,
    in_recv,
    edge_send,
    main_send,
    main_recv,
    relay_send,
    relay_recv,
    ready,
):
    around = directions(sizes)
    sections, rows, cols = sizes
    batch, height, width, chans = latent.shape
    half = height * 5 // 8
    least = half - (sections - 1)
    s = lax.axis_index("section")
    r = lax.axis_index("row")
    c = lax.axis_index("col")
    first = s == 0
    relays = sections > 3
    origin, relay = relays & (s == 1), relays & (s == 3)
    feeds = s + 1 < sections
    odd = lax.rem(r, 2)
    step = 1 - 2 * odd

    def line(y):
        return y + odd * (height - 1 - 2 * y)

    def ordered(source, b, y0, y1):
        return jnp.stack([source[b, line(y)] for y in range(y0, y1)])

    def opposite(d):
        dr, dc = around[d]
        return around.index((dr, -dc))

    def inside(dr, dc):
        return (r + dr * step >= 0) & (r + dr * step < rows) & (c + dc >= 0) & (c + dc < cols)

    def at(ds, dr, dc):
        return (s + ds, r + dr * step, c + dc)

    def taps_of(dy, start):
        return weights_hbm.at[0, pl.ds(3 * (dy + odd * (2 - 2 * dy)), 3), pl.ds(start, chans)]

    loads = [
        pltpu.make_async_copy(src, dst, load_sem.at[k])
        for k, (src, dst) in enumerate(
            [(hidden_hbm.at[0], hidden), (latent_hbm, latent)]
            + [(taps_of(dy, chans), w_own.at[pl.ds(3 * dy, 3)]) for dy in range(3)]
            + [(taps_of(dy, 0), w_in.at[pl.ds(3 * dy, 3)]) for dy in range(3)]
            + [(cell_hbm.at[0], cell)]
        )
    ]
    for load in loads[:2]:
        load.start()

    halo_in[...] = jnp.zeros_like(halo_in)
    corner_in[...] = jnp.zeros_like(corner_in)
    halo_own[...] = jnp.zeros_like(halo_own)
    wide[...] = jnp.zeros_like(wide)
    halo_lat[...] = jnp.zeros_like(halo_lat)

    barrier = pltpu.get_barrier_semaphore()
    expected = jnp.int32(0)
    listeners = jnp.int32(0)
    for dr, dc in around + ((0, 0),):
        there = inside(dr, dc)
        if (dr, dc) != (0, 0):

            @pl.when(there)
            def _():
                pl.semaphore_signal(barrier, inc=1, device_id=at(0, dr, dc), device_id_type=MESH)

            expected = expected + there.astype(jnp.int32)

    for dr, dc in around + ((0, 0),):
        there = inside(dr, dc)

        @pl.when(there & feeds)
        def _():
            pl.semaphore_signal(barrier, inc=1, device_id=at(1, dr, dc), device_id_type=MESH)

        expected = expected + (there & (s > 0)).astype(jnp.int32)
        listeners = listeners + (there & feeds).astype(jnp.int32)

    @pl.when(origin)
    def _():
        pl.semaphore_signal(barrier, inc=1, device_id=at(2, 0, 0), device_id_type=MESH)

    expected = expected + relay.astype(jnp.int32)
    listeners = listeners + origin.astype(jnp.int32)

    for load in loads[2:]:
        load.start()

    def pack(source, edges, b):
        tile = ordered(source, b, 0, height).astype(F32)
        edges[0, b] = tile[:, 0, :].astype(BF16)
        edges[1, b] = tile[:, width - 1, :].astype(BF16)

    loads[0].wait()
    for b in range(batch):
        pack(hidden, own_edges, b)
    loads[1].wait()

    @pl.when(first)
    def _():
        for b in range(batch):
            pack(latent, lat_edges, b)

    pl.semaphore_wait(barrier, expected)

    for dr, dc in around + ((0, 0),):

        @pl.when(inside(dr, dc) & (s > 0))
        def _():
            pl.semaphore_signal(ready, inc=1, device_id=at(-1, dr, dc), device_id_type=MESH)

    @pl.when(relay)
    def _():
        pl.semaphore_signal(ready, inc=1, device_id=at(-2, 0, 0), device_id_type=MESH)

    def edge(tile, edges, dr, dc):
        if dr == 0:
            return edges.at[0 if dc < 0 else 1]
        return tile.at[:, line(0 if dr < 0 else height - 1)]

    def own_copy(d):
        dr, dc = around[d]
        back = opposite(d)
        return pltpu.make_async_remote_copy(
            src_ref=edge(hidden, own_edges, dr, dc),
            dst_ref=halo_own.at[back],
            send_sem=own_send.at[d],
            recv_sem=own_recv.at[back],
            device_id=at(0, dr, dc),
            device_id_type=MESH,
        )

    def lat_copy(d):
        dr, dc = around[d]
        back = opposite(d)
        return pltpu.make_async_remote_copy(
            src_ref=edge(latent, lat_edges, dr, dc),
            dst_ref=halo_lat.at[back],
            send_sem=lat_send.at[d],
            recv_sem=lat_recv.at[back],
            device_id=at(0, dr, dc),
            device_id_type=MESH,
        )

    def edge_copy(d, b, part):
        dr, dc = around[d]
        back = opposite(d)
        if dr == 0:
            src, dst = new_edges.at[0 if dc < 0 else 1, b, part], halo_in.at[back, b, part]
        elif dc == 0:
            src, dst = new_hidden.at[b, 0 if dr < 0 else height - 1], halo_in.at[back, b, part]
        else:
            src, dst = new_corners.at[0 if dc < 0 else 1, b, part], corner_in.at[back, b]
        return pltpu.make_async_remote_copy(
            src_ref=src,
            dst_ref=dst,
            send_sem=edge_send.at[d, b, part],
            recv_sem=in_recv.at[back, b, part],
            device_id=at(1, dr, dc),
            device_id_type=MESH,
        )

    def extent(section, part):
        cut = half - section
        return (0, cut) if part == 0 else (cut, height)

    def middle(part):
        y0, y1 = extent(1, part)
        return y0 + (y1 - y0) * 2 // 5

    def relay_copy(b, part, leg):
        y0 = extent(1, part)[0]
        span = pl.ds(y0, middle(part) - y0)
        src, dst = ((new_hidden, passing), (passing, main_in))[leg]
        return pltpu.make_async_remote_copy(
            src_ref=src.at[b, span],
            dst_ref=dst.at[b, span],
            send_sem=relay_send.at[leg, b, part],
            recv_sem=relay_recv.at[leg, b, part],
            device_id=at(2 if leg == 0 else -1, 0, 0),
            device_id_type=MESH,
        )

    def main_copy(b, part, section):
        y0, y1 = extent(section, part)
        if relays and section == 1:
            y0 = middle(part)
        span = pl.ds(y0, y1 - y0)
        return pltpu.make_async_remote_copy(
            src_ref=new_hidden.at[b, span],
            dst_ref=main_in.at[b, span],
            send_sem=main_send.at[b, part],
            recv_sem=main_recv.at[b, part],
            device_id=at(1, 0, 0),
            device_id_type=MESH,
        )

    def in_part(d, part):
        dr = around[d][0]
        return dr == 0 or (dr < 0) == (part == 0)

    for d, (dr, dc) in enumerate(around):

        @pl.when(inside(dr, dc) & first)
        def _():
            lat_copy(d).start()

    for d, (dr, dc) in enumerate(around):

        @pl.when(inside(dr, dc))
        def _():
            own_copy(d).start()

    left, right = PAD - 1, PAD + width

    def put_side(dc, y0, y1, strip):
        side = left if dc < 0 else right
        wide[1 + y0 : 1 + y1, side : side + 1, :] = strip.reshape(y1 - y0, 1, chans)

    def put_line(dr, strip):
        wide[0 if dr < 0 else height + 1, PAD : PAD + width, :] = strip

    def put_tile(source, b):
        for y in range(height):
            wide[1 + y, PAD : PAD + width, :] = source[b, line(y)].astype(F32)

    def convolved(y0, y1, w):
        for dx in range(3):
            taps[y0 : y1 + 2, :, dx * chans : (dx + 1) * chans] = wide[
                y0 : y1 + 2, left + dx : left + dx + width, :
            ].astype(BF16)
        patch = jnp.concatenate(
            [
                taps[y0 + dy : y1 + dy].reshape((y1 - y0) * width, 3 * chans)
                for dy in range(3)
            ],
            axis=-1,
        )
        return jnp.dot(patch, w[...].reshape(9 * chans, -1), preferred_element_type=F32)

    def add_borders(halo, w):
        side_cells = height
        for d, (dr, dc) in enumerate(around):
            if dr != 0 and dc != 0:
                continue
            border[:, PAD : PAD + side_cells, :] = halo[d].astype(F32)
            for end, place in ((-1, PAD - 1), (1, PAD + side_cells)):
                if dr == 0 and (end, dc) in around:
                    x = width - 1 if dc < 0 else 0
                    corner = halo[around.index((end, dc))].astype(F32)[:, x : x + 1, :]
                else:
                    corner = jnp.zeros((batch, 1, chans), F32)
                border[:, place : place + 1, :] = corner
            patch = jnp.concatenate(
                [
                    border[:, PAD - 1 + k : PAD - 1 + k + side_cells, :].reshape(-1, chans)
                    for k in range(3)
                ],
                axis=-1,
            ).astype(BF16)
            if dr == 0:
                part_w = jnp.concatenate([w[3 * k + 1 + dc] for k in range(3)], axis=0)
            else:
                part_w = w[3 + 3 * dr : 6 + 3 * dr].reshape(3 * chans, -1)
            more = jnp.dot(patch, part_w, preferred_element_type=F32)
            more = more.reshape(batch, side_cells, -1)
            if dr == 0:
                x = 0 if dc < 0 else width - 1
                for b in range(batch):
                    gates[b, :, x, :] += more[b]
            else:
                gates[:, 0 if dr < 0 else height - 1] += more

    for load in loads[2:5]:
        load.wait()
    for b in range(batch):
        put_tile(hidden, b)
        gates[b] = (convolved(0, height, w_own) + bias_ref[...]).reshape(height, width, -1)
    for load in loads[5:8]:
        load.wait()

    @pl.when(first)
    def _():
        for b in range(batch):
            put_tile(latent, b)
            gates[b] += convolved(0, height, w_in).reshape(height, width, -1)

        for d, (dr, dc) in enumerate(around):

            @pl.when(inside(dr, dc))
            def _():
                lat_copy(opposite(d)).wait_recv()

        add_borders(halo_lat, w_in)

    for d, (dr, dc) in enumerate(around):

        @pl.when(inside(dr, dc))
        def _():
            own_copy(opposite(d)).wait_recv()

    add_borders(halo_own, w_own)
    loads[8].wait()

    if relays:

        @pl.when(relay)
        def _():
            for b in range(batch):
                for part in range(2):
                    relay_copy(b, part, 0).wait_recv()
                    relay_copy(b, part, 1).start()

    stores = []
    for b in range(batch):
        for part in range(2):
            y0, y1 = (0, half) if part == 0 else (least, height)

            @pl.when(s > 0)
            def _():
                for d, (dr, dc) in enumerate(around):
                    if in_part(d, part):

                        @pl.when(inside(dr, dc))
                        def _():
                            edge_copy(opposite(d), b, part).wait_recv()

                        if dr == 0:
                            strip = halo_in[d, b, part].astype(F32)
                            put_side(dc, y0, y1, strip[: y1 - y0])
                        elif dc == 0:
                            put_line(dr, halo_in[d, b, part].astype(F32))
                        else:
                            y, side = 0 if dr < 0 else height + 1, left if dc < 0 else right
                            wide[y, side : side + 1, :] = corner_in[d, b]

            for section in range(1, sections):

                @pl.when(s == section)
                def _():
                    main_copy(b, part, section - 1).wait_recv()
                    if relays and section == 2:
                        relay_copy(b, part, 1).wait_recv()
                    m0, m1 = extent(section - 1, part)
                    wide[1 + m0 : 1 + m1, PAD : PAD + width, :] = main_in[b, m0:m1].astype(F32)

            count = (y1 - y0) * width

            @pl.when(first)
            def _():
                total[:count] = gates[b, y0:y1].reshape(count, -1)

            @pl.when(s > 0)
            def _():
                total[:count] = gates[b, y0:y1].reshape(count, -1) + convolved(y0, y1, w_in)

            z = total[:count]
            old = ordered(cell, b, y0, y1).reshape(count, chans)
            gate_i = sigmoid(z[:, :chans])
            gate_f = sigmoid(z[:, chans : 2 * chans])
            gate_g = jnp.tanh(z[:, 2 * chans : 3 * chans])
            gate_o = sigmoid(z[:, 3 * chans :])
            keep, add = gate_f * old, gate_i * gate_g
            now = keep + add
            out = (gate_o * jnp.tanh(now)).astype(BF16).reshape(y1 - y0, width, chans)

            for y in range(y0, y1):
                if part == 0 or y >= half:
                    new_hidden[b, y] = out[y - y0]
                else:

                    @pl.when(y >= half - s)
                    def _():
                        new_hidden[b, y] = out[y - y0]

            tile = out.astype(F32)
            spare = jnp.zeros((height - (y1 - y0), chans), F32)
            for side, x in enumerate((0, width - 1)):
                new_edges[side, b, part] = jnp.concatenate([tile[:, x, :], spare]).astype(BF16)
                y = 0 if part == 0 else y1 - y0 - 1
                new_corners[side, b, part] = tile[y, x : x + 1, :]

            if b == 0 and part == 0:

                @pl.when(feeds)
                def _():
                    pl.semaphore_wait(ready, listeners)

            for d, (dr, dc) in enumerate(around):
                if in_part(d, part):

                    @pl.when(inside(dr, dc) & feeds)
                    def _():
                        edge_copy(d, b, part).start()

            for section in range(sections - 1):

                @pl.when(s == section)
                def _():
                    if relays and section == 1:
                        relay_copy(b, part, 0).start()
                    main_copy(b, part, section).start()

            for value, ref in ((keep, kept), (add, added), (gate_o, opened)):
                value = value.reshape(y1 - y0, width, chans)
                for y in range(y0, y1):
                    ref[b, line(y)] = value[y - y0]

        for k, (src, dst) in enumerate(
            ((kept, kept_out), (added, added_out), (opened, opened_out))
        ):
            store = pltpu.make_async_copy(src.at[b], dst.at[0, b], store_sem.at[k, b])
            store.start()
            stores.append(store)

    for d, (dr, dc) in enumerate(around):

        @pl.when(inside(dr, dc))
        def _():
            own_copy(d).wait_send()

        @pl.when(inside(dr, dc) & first)
        def _():
            lat_copy(d).wait_send()

    for b in range(batch):
        for d, (dr, dc) in enumerate(around):
            for part in range(2):
                if in_part(d, part):

                    @pl.when(inside(dr, dc) & feeds)
                    def _():
                        edge_copy(d, b, part).wait_send()

        for part in range(2):
            for section in range(sections - 1):

                @pl.when(s == section)
                def _():
                    main_copy(b, part, section).wait_send()
                    if relays and section == 1:
                        relay_copy(b, part, 0).wait_send()

    if relays:

        @pl.when(relay)
        def _():
            for b in range(batch):
                for part in range(2):
                    relay_copy(b, part, 1).wait_send()

    for store in stores:
        store.wait()


def on_device(latent, hidden_old, cell_old, weights, bias):
    sizes = tuple(lax.axis_size(axis) for axis in ("section", "row", "col"))
    batch, height, width, chans = latent.shape
    gate_chans = weights.shape[-1]
    around = len(directions(sizes))
    edge = max(height, width)
    assert height == width and height % 16 == 0 and sizes[0] < height // 2
    tile = (batch, height, width, chans)
    dma = pltpu.SemaphoreType.DMA
    anywhere = pl.BlockSpec(memory_space=pltpu.HBM)
    flops = 2 * batch * height * width * 9 * 2 * chans * gate_chans
    kept, added, opened = pl.pallas_call(
        functools.partial(kernel, sizes),
        out_shape=(jax.ShapeDtypeStruct(cell_old.shape, F32),) * 3,
        in_specs=[anywhere] * 4 + [pl.BlockSpec(memory_space=pltpu.VMEM)],
        out_specs=(anywhere,) * 3,
        scratch_shapes=[
            pltpu.VMEM(tile, BF16),
            pltpu.VMEM(tile, BF16),
            pltpu.VMEM(tile, F32),
            pltpu.VMEM((9, chans, gate_chans), BF16),
            pltpu.VMEM((9, chans, gate_chans), BF16),
            pltpu.VMEM(tile, BF16),
            pltpu.VMEM(tile, BF16),
            pltpu.VMEM((around, batch, 2, edge, chans), BF16),
            pltpu.VMEM((around, batch, 1, chans), F32),
            pltpu.VMEM((2, batch, 2, 1, chans), F32),
            pltpu.VMEM((around, batch, edge, chans), BF16),
            pltpu.VMEM((around, batch, edge, chans), BF16),
            pltpu.VMEM((2, batch, edge, chans), BF16),
            pltpu.VMEM((2, batch, edge, chans), BF16),
            pltpu.VMEM((2, batch, 2, edge, chans), BF16),
            pltpu.VMEM(tile, BF16),
            pltpu.VMEM(tile, F32),
            pltpu.VMEM(tile, F32),
            pltpu.VMEM(tile, F32),
            pltpu.VMEM((height + 2, width + 2 * PAD, chans), F32),
            pltpu.VMEM((height + 2, width, 3 * chans), BF16),
            pltpu.VMEM((batch, edge + 2 * PAD, chans), F32),
            pltpu.VMEM((batch, height, width, gate_chans), F32),
            pltpu.VMEM((height * width, gate_chans), F32),
            dma((9,)),
            dma((3, batch)),
            dma((around,)),
            dma((around,)),
            dma((around,)),
            dma((around,)),
            dma((around, batch, 2)),
            dma((around, batch, 2)),
            dma((batch, 2)),
            dma((batch, 2)),
            dma((2, batch, 2)),
            dma((2, batch, 2)),
            pltpu.SemaphoreType.REGULAR,
        ],
        compiler_params=pltpu.CompilerParams(
            collective_id=0, has_side_effects=True, vmem_limit_bytes=64 * 1024 * 1024 - 4096
        ),
        cost_estimate=pl.CostEstimate(
            flops=flops, bytes_accessed=weights.size * 2, transcendentals=0
        ),
    )(latent, hidden_old, cell_old, weights, bias)
    cell = kept + added
    return (opened * jnp.tanh(cell)).astype(BF16), cell


def solution(mesh):
    in_specs = (
        P(None, "row", "col", None),
        P("section", None, "row", "col", None),
        P("section", None, "row", "col", None),
        P("section", None, None, None),
        P("section", None),
    )
    out_specs = (P("section", None, "row", "col", None), P("section", None, "row", "col", None))
    return jax.shard_map(
        on_device, mesh=mesh, in_specs=in_specs, out_specs=out_specs, check_vma=False
    )
```

```python
import functools

import jax
import jax.numpy as jnp
from jax import lax
from jax.experimental import pallas as pl
from jax.experimental.pallas import tpu as pltpu
from jax.sharding import PartitionSpec as P

MESH = pl.DeviceIdType.MESH
F32 = jnp.float32
BF16 = jnp.bfloat16
PAD = 8


def directions(sizes):
    across = (-1, 0, 1) if sizes[1] > 2 else (0, 1) if sizes[1] > 1 else (0,)
    along = (-1, 0, 1) if sizes[2] > 1 else (0,)
    return tuple((dr, dc) for dr in across for dc in along if (dr, dc) != (0, 0))


def sigmoid(x):
    return 0.5 * jnp.tanh(0.5 * x) + 0.5


def kernel(
    sizes,
    latent_hbm,
    hidden_hbm,
    cell_hbm,
    weights_hbm,
    bias_ref,
    kept_out,
    added_out,
    opened_out,
    latent,
    hidden,
    cell,
    w_in,
    w_own,
    main_in,
    halo_in,
    corner_in,
    new_corners,
    halo_own,
    halo_lat,
    own_edges,
    lat_edges,
    new_edges,
    new_hidden,
    kept,
    added,
    opened,
    wide,
    taps,
    border,
    gates,
    total,
    load_sem,
    store_sem,
    own_send,
    own_recv,
    lat_send,
    lat_recv,
    in_recv,
    edge_send,
    main_send,
    main_recv,
    ready,
):
    around = directions(sizes)
    sections, rows, cols = sizes
    batch, height, width, chans = latent.shape
    half = height * 5 // 8
    least = half - (sections - 1)
    s = lax.axis_index("section")
    r = lax.axis_index("row")
    c = lax.axis_index("col")
    first = s == 0
    feeds = s + 1 < sections
    odd = lax.rem(r, 2)
    step = 1 - 2 * odd

    def line(y):
        return y + odd * (height - 1 - 2 * y)

    def ordered(source, b, y0, y1):
        return jnp.stack([source[b, line(y)] for y in range(y0, y1)])

    def opposite(d):
        dr, dc = around[d]
        return around.index((dr, -dc))

    def inside(dr, dc):
        return (r + dr * step >= 0) & (r + dr * step < rows) & (c + dc >= 0) & (c + dc < cols)

    def at(ds, dr, dc):
        return (s + ds, r + dr * step, c + dc)

    def taps_of(dy, start):
        return weights_hbm.at[0, pl.ds(3 * (dy + odd * (2 - 2 * dy)), 3), pl.ds(start, chans)]

    loads = [
        pltpu.make_async_copy(src, dst, load_sem.at[k])
        for k, (src, dst) in enumerate(
            [(hidden_hbm.at[0], hidden), (latent_hbm, latent)]
            + [(taps_of(dy, chans), w_own.at[pl.ds(3 * dy, 3)]) for dy in range(3)]
            + [(taps_of(dy, 0), w_in.at[pl.ds(3 * dy, 3)]) for dy in range(3)]
            + [(cell_hbm.at[0], cell)]
        )
    ]
    for load in loads[:2]:
        load.start()

    halo_in[...] = jnp.zeros_like(halo_in)
    corner_in[...] = jnp.zeros_like(corner_in)
    halo_own[...] = jnp.zeros_like(halo_own)
    wide[...] = jnp.zeros_like(wide)
    halo_lat[...] = jnp.zeros_like(halo_lat)

    barrier = pltpu.get_barrier_semaphore()
    expected = jnp.int32(0)
    listeners = jnp.int32(0)
    for dr, dc in around + ((0, 0),):
        there = inside(dr, dc)
        if (dr, dc) != (0, 0):

            @pl.when(there)
            def _():
                pl.semaphore_signal(barrier, inc=1, device_id=at(0, dr, dc), device_id_type=MESH)

            expected = expected + there.astype(jnp.int32)

    for dr, dc in around + ((0, 0),):
        there = inside(dr, dc)

        @pl.when(there & feeds)
        def _():
            pl.semaphore_signal(barrier, inc=1, device_id=at(1, dr, dc), device_id_type=MESH)

        expected = expected + (there & (s > 0)).astype(jnp.int32)
        listeners = listeners + (there & feeds).astype(jnp.int32)

    for load in loads[2:]:
        load.start()

    def pack(source, edges, b):
        tile = ordered(source, b, 0, height).astype(F32)
        edges[0, b] = tile[:, 0, :].astype(BF16)
        edges[1, b] = tile[:, width - 1, :].astype(BF16)

    loads[0].wait()
    for b in range(batch):
        pack(hidden, own_edges, b)
    loads[1].wait()

    @pl.when(first)
    def _():
        for b in range(batch):
            pack(latent, lat_edges, b)

    pl.semaphore_wait(barrier, expected)

    for dr, dc in around + ((0, 0),):

        @pl.when(inside(dr, dc) & (s > 0))
        def _():
            pl.semaphore_signal(ready, inc=1, device_id=at(-1, dr, dc), device_id_type=MESH)

    def edge(tile, edges, dr, dc):
        if dr == 0:
            return edges.at[0 if dc < 0 else 1]
        return tile.at[:, line(0 if dr < 0 else height - 1)]

    def own_copy(d):
        dr, dc = around[d]
        back = opposite(d)
        return pltpu.make_async_remote_copy(
            src_ref=edge(hidden, own_edges, dr, dc),
            dst_ref=halo_own.at[back],
            send_sem=own_send.at[d],
            recv_sem=own_recv.at[back],
            device_id=at(0, dr, dc),
            device_id_type=MESH,
        )

    def lat_copy(d):
        dr, dc = around[d]
        back = opposite(d)
        return pltpu.make_async_remote_copy(
            src_ref=edge(latent, lat_edges, dr, dc),
            dst_ref=halo_lat.at[back],
            send_sem=lat_send.at[d],
            recv_sem=lat_recv.at[back],
            device_id=at(0, dr, dc),
            device_id_type=MESH,
        )

    def edge_copy(d, b, part):
        dr, dc = around[d]
        back = opposite(d)
        if dr == 0:
            src, dst = new_edges.at[0 if dc < 0 else 1, b, part], halo_in.at[back, b, part]
        elif dc == 0:
            src, dst = new_hidden.at[b, 0 if dr < 0 else height - 1], halo_in.at[back, b, part]
        else:
            src, dst = new_corners.at[0 if dc < 0 else 1, b, part], corner_in.at[back, b]
        return pltpu.make_async_remote_copy(
            src_ref=src,
            dst_ref=dst,
            send_sem=edge_send.at[d, b, part],
            recv_sem=in_recv.at[back, b, part],
            device_id=at(1, dr, dc),
            device_id_type=MESH,
        )

    def extent(section, part):
        cut = half - section
        return (0, cut) if part == 0 else (cut, height)

    def main_copy(b, part, section):
        y0, y1 = extent(section, part)
        span = pl.ds(y0, y1 - y0)
        return pltpu.make_async_remote_copy(
            src_ref=new_hidden.at[b, span],
            dst_ref=main_in.at[b, span],
            send_sem=main_send.at[b, part],
            recv_sem=main_recv.at[b, part],
            device_id=at(1, 0, 0),
            device_id_type=MESH,
        )

    def in_part(d, part):
        dr = around[d][0]
        return dr == 0 or (dr < 0) == (part == 0)

    for d, (dr, dc) in enumerate(around):

        @pl.when(inside(dr, dc) & first)
        def _():
            lat_copy(d).start()

    for d, (dr, dc) in enumerate(around):

        @pl.when(inside(dr, dc))
        def _():
            own_copy(d).start()

    left, right = PAD - 1, PAD + width

    def put_side(dc, y0, y1, strip):
        side = left if dc < 0 else right
        wide[1 + y0 : 1 + y1, side : side + 1, :] = strip.reshape(y1 - y0, 1, chans)

    def put_line(dr, strip):
        wide[0 if dr < 0 else height + 1, PAD : PAD + width, :] = strip

    def put_tile(source, b):
        for y in range(height):
            wide[1 + y, PAD : PAD + width, :] = source[b, line(y)].astype(F32)

    def convolved(y0, y1, w):
        for dx in range(3):
            taps[y0 : y1 + 2, :, dx * chans : (dx + 1) * chans] = wide[
                y0 : y1 + 2, left + dx : left + dx + width, :
            ].astype(BF16)
        patch = jnp.concatenate(
            [
                taps[y0 + dy : y1 + dy].reshape((y1 - y0) * width, 3 * chans)
                for dy in range(3)
            ],
            axis=-1,
        )
        return jnp.dot(patch, w[...].reshape(9 * chans, -1), preferred_element_type=F32)

    def add_borders(halo, w):
        side_cells = height
        for d, (dr, dc) in enumerate(around):
            if dr != 0 and dc != 0:
                continue
            border[:, PAD : PAD + side_cells, :] = halo[d].astype(F32)
            for end, place in ((-1, PAD - 1), (1, PAD + side_cells)):
                if dr == 0 and (end, dc) in around:
                    x = width - 1 if dc < 0 else 0
                    corner = halo[around.index((end, dc))].astype(F32)[:, x : x + 1, :]
                else:
                    corner = jnp.zeros((batch, 1, chans), F32)
                border[:, place : place + 1, :] = corner
            patch = jnp.concatenate(
                [
                    border[:, PAD - 1 + k : PAD - 1 + k + side_cells, :].reshape(-1, chans)
                    for k in range(3)
                ],
                axis=-1,
            ).astype(BF16)
            if dr == 0:
                part_w = jnp.concatenate([w[3 * k + 1 + dc] for k in range(3)], axis=0)
            else:
                part_w = w[3 + 3 * dr : 6 + 3 * dr].reshape(3 * chans, -1)
            more = jnp.dot(patch, part_w, preferred_element_type=F32)
            more = more.reshape(batch, side_cells, -1)
            if dr == 0:
                x = 0 if dc < 0 else width - 1
                for b in range(batch):
                    gates[b, :, x, :] += more[b]
            else:
                gates[:, 0 if dr < 0 else height - 1] += more

    for load in loads[2:5]:
        load.wait()
    gates[...] = jnp.broadcast_to(bias_ref[...].reshape(1, 1, 1, -1), gates.shape)

    def add_own(b):
        put_tile(hidden, b)
        gates[b] += convolved(0, height, w_own).reshape(height, width, -1)

    def add_latent(b):
        put_tile(latent, b)
        gates[b] += convolved(0, height, w_in).reshape(height, width, -1)

    add_own(0)

    @pl.when(s > 0)
    def _():
        for b in range(1, batch):
            add_own(b)

    for load in loads[5:8]:
        load.wait()

    @pl.when(first)
    def _():
        add_latent(0)

        for d, (dr, dc) in enumerate(around):

            @pl.when(inside(dr, dc))
            def _():
                lat_copy(opposite(d)).wait_recv()

        add_borders(halo_lat, w_in)

    for d, (dr, dc) in enumerate(around):

        @pl.when(inside(dr, dc))
        def _():
            own_copy(opposite(d)).wait_recv()

    add_borders(halo_own, w_own)
    loads[8].wait()

    stores = []
    for b in range(batch):
        if b > 0:

            @pl.when(first)
            def _():
                add_own(b)
                add_latent(b)

        for part in range(2):
            y0, y1 = (0, half) if part == 0 else (least, height)

            @pl.when(s > 0)
            def _():
                for d, (dr, dc) in enumerate(around):
                    if in_part(d, part):

                        @pl.when(inside(dr, dc))
                        def _():
                            edge_copy(opposite(d), b, part).wait_recv()

                        if dr == 0:
                            strip = halo_in[d, b, part].astype(F32)
                            put_side(dc, y0, y1, strip[: y1 - y0])
                        elif dc == 0:
                            put_line(dr, halo_in[d, b, part].astype(F32))
                        else:
                            y, side = 0 if dr < 0 else height + 1, left if dc < 0 else right
                            wide[y, side : side + 1, :] = corner_in[d, b]

            for section in range(1, sections):

                @pl.when(s == section)
                def _():
                    main_copy(b, part, section - 1).wait_recv()
                    m0, m1 = extent(section - 1, part)
                    wide[1 + m0 : 1 + m1, PAD : PAD + width, :] = main_in[b, m0:m1].astype(F32)

            count = (y1 - y0) * width

            @pl.when(first)
            def _():
                total[:count] = gates[b, y0:y1].reshape(count, -1)

            @pl.when(s > 0)
            def _():
                total[:count] = gates[b, y0:y1].reshape(count, -1) + convolved(y0, y1, w_in)

            z = total[:count]
            old = ordered(cell, b, y0, y1).reshape(count, chans)
            gate_i = sigmoid(z[:, :chans])
            gate_f = sigmoid(z[:, chans : 2 * chans])
            gate_g = jnp.tanh(z[:, 2 * chans : 3 * chans])
            gate_o = sigmoid(z[:, 3 * chans :])
            keep, add = gate_f * old, gate_i * gate_g
            now = keep + add
            out = (gate_o * jnp.tanh(now)).astype(BF16).reshape(y1 - y0, width, chans)

            for y in range(y0, y1):
                if part == 0 or y >= half:
                    new_hidden[b, y] = out[y - y0]
                else:

                    @pl.when(y >= half - s)
                    def _():
                        new_hidden[b, y] = out[y - y0]

            tile = out.astype(F32)
            spare = jnp.zeros((height - (y1 - y0), chans), F32)
            for side, x in enumerate((0, width - 1)):
                new_edges[side, b, part] = jnp.concatenate([tile[:, x, :], spare]).astype(BF16)
                y = 0 if part == 0 else y1 - y0 - 1
                new_corners[side, b, part] = tile[y, x : x + 1, :]

            if b == 0 and part == 0:

                @pl.when(feeds)
                def _():
                    pl.semaphore_wait(ready, listeners)

            for d, (dr, dc) in enumerate(around):
                if in_part(d, part):

                    @pl.when(inside(dr, dc) & feeds)
                    def _():
                        edge_copy(d, b, part).start()

            for section in range(sections - 1):

                @pl.when(s == section)
                def _():
                    main_copy(b, part, section).start()

            for value, ref in ((keep, kept), (add, added), (gate_o, opened)):
                value = value.reshape(y1 - y0, width, chans)
                for y in range(y0, y1):
                    ref[b, line(y)] = value[y - y0]

        for k, (src, dst) in enumerate(
            ((kept, kept_out), (added, added_out), (opened, opened_out))
        ):
            store = pltpu.make_async_copy(src.at[b], dst.at[0, b], store_sem.at[k, b])
            store.start()
            stores.append(store)

    for d, (dr, dc) in enumerate(around):

        @pl.when(inside(dr, dc))
        def _():
            own_copy(d).wait_send()

        @pl.when(inside(dr, dc) & first)
        def _():
            lat_copy(d).wait_send()

    for b in range(batch):
        for d, (dr, dc) in enumerate(around):
            for part in range(2):
                if in_part(d, part):

                    @pl.when(inside(dr, dc) & feeds)
                    def _():
                        edge_copy(d, b, part).wait_send()

        for part in range(2):
            for section in range(sections - 1):

                @pl.when(s == section)
                def _():
                    main_copy(b, part, section).wait_send()

    for store in stores:
        store.wait()


def on_device(latent, hidden_old, cell_old, weights, bias):
    sizes = tuple(lax.axis_size(axis) for axis in ("section", "row", "col"))
    batch, height, width, chans = latent.shape
    gate_chans = weights.shape[-1]
    around = len(directions(sizes))
    edge = max(height, width)
    assert height == width and height % 16 == 0 and sizes[0] < height // 2
    tile = (batch, height, width, chans)
    dma = pltpu.SemaphoreType.DMA
    anywhere = pl.BlockSpec(memory_space=pltpu.HBM)
    flops = 2 * batch * height * width * 9 * 2 * chans * gate_chans
    kept, added, opened = pl.pallas_call(
        functools.partial(kernel, sizes),
        out_shape=(jax.ShapeDtypeStruct(cell_old.shape, F32),) * 3,
        in_specs=[anywhere] * 4 + [pl.BlockSpec(memory_space=pltpu.VMEM)],
        out_specs=(anywhere,) * 3,
        scratch_shapes=[
            pltpu.VMEM(tile, BF16),
            pltpu.VMEM(tile, BF16),
            pltpu.VMEM(tile, F32),
            pltpu.VMEM((9, chans, gate_chans), BF16),
            pltpu.VMEM((9, chans, gate_chans), BF16),
            pltpu.VMEM(tile, BF16),
            pltpu.VMEM((around, batch, 2, edge, chans), BF16),
            pltpu.VMEM((around, batch, 1, chans), F32),
            pltpu.VMEM((2, batch, 2, 1, chans), F32),
            pltpu.VMEM((around, batch, edge, chans), BF16),
            pltpu.VMEM((around, batch, edge, chans), BF16),
            pltpu.VMEM((2, batch, edge, chans), BF16),
            pltpu.VMEM((2, batch, edge, chans), BF16),
            pltpu.VMEM((2, batch, 2, edge, chans), BF16),
            pltpu.VMEM(tile, BF16),
            pltpu.VMEM(tile, F32),
            pltpu.VMEM(tile, F32),
            pltpu.VMEM(tile, F32),
            pltpu.VMEM((height + 2, width + 2 * PAD, chans), F32),
            pltpu.VMEM((height + 2, width, 3 * chans), BF16),
            pltpu.VMEM((batch, edge + 2 * PAD, chans), F32),
            pltpu.VMEM((batch, height, width, gate_chans), F32),
            pltpu.VMEM((height * width, gate_chans), F32),
            dma((9,)),
            dma((3, batch)),
            dma((around,)),
            dma((around,)),
            dma((around,)),
            dma((around,)),
            dma((around, batch, 2)),
            dma((around, batch, 2)),
            dma((batch, 2)),
            dma((batch, 2)),
            pltpu.SemaphoreType.REGULAR,
        ],
        compiler_params=pltpu.CompilerParams(
            collective_id=0, has_side_effects=True, vmem_limit_bytes=64 * 1024 * 1024 - 4096
        ),
        cost_estimate=pl.CostEstimate(
            flops=flops, bytes_accessed=weights.size * 2, transcendentals=0
        ),
    )(latent, hidden_old, cell_old, weights, bias)
    cell = kept + added
    return (opened * jnp.tanh(cell)).astype(BF16), cell


def solution(mesh):
    in_specs = (
        P(None, "row", "col", None),
        P("section", None, "row", "col", None),
        P("section", None, "row", "col", None),
        P("section", None, None, None),
        P("section", None),
    )
    out_specs = (P("section", None, "row", "col", None), P("section", None, "row", "col", None))
    return jax.shard_map(
        on_device, mesh=mesh, in_specs=in_specs, out_specs=out_specs, check_vma=False
    )
```
